128 devices in a mesh: role: 2 (over core), batch: 8 (over x_lo, z), tensor: 8 (over y, x_hi).
Axes of the slice: x: 4 (x_hi: 2, x_lo: 2; x = x_hi * 2 + x_lo), y: 4, z: 4, core: 2. Of those that a mesh axis runs over, the one named last changes fastest.
Arguments:
- span_x: bfloat16 [8192, 8192], P('batch'), may hold values from -40 to 40
- norm_gain: bfloat16 [8192], replicated, may hold values from 0.099609375 to 1.8984375
- key_value_weight: bfloat16 [8192, 8, 2, 128], P(None, 'tensor', 'role'), may hold values from -0.0625 to 0.0625
- key_value_bias: bfloat16 [8, 2, 128], P('tensor', 'role'), may hold values from -4 to 4
- queries: bfloat16 [4, 256, 64, 128], P(None, ('role', 'batch'), 'tensor'), may hold values from -200 to 200
- decode_key_value: bfloat16 [4, 256, 8, 2, 128], P(None, ('role', 'batch'), 'tensor'), may hold values from -4 to 4
- kv_cache: bfloat16 [256, 256, 8, 2, 128], P(('role', 'batch'), None, 'tensor'), may hold values from -4 to 4
- w_out: bfloat16 [8192, 8192], P('tensor', ('role', 'batch')), may hold values from -0.5 to 0.5
- members: int32 [256], replicated, may hold values from 0 to 255, as said below
- span_req: int32 [8192], replicated, may hold values from 0 to 255, as said below
- span_pos: int32 [8192], replicated, may hold values from 2 to 767, as said below
- cache_len: int32 [256], replicated, may hold values from 2 to 256, as said below
Outputs:
- layer_output: bfloat16 [256, 4, 8192], P('tensor', None, ('role', 'batch'))
The draws below stay inside these ranges and needn't reach their ends.
Inputs may be any that keep to these rules, and one draw needn't show every extreme that they name: `members`: A permutation: each request sits in exactly one decode slot; decode owner o holds slots o * 16 to o * 16 + 15. `span_req`: in every block of 1024 consecutive span tokens, exactly 64 tokens belong to the requests of each decode owner. `span_pos`: the span tokens of request r take, in span order, the positions cache_len[r], cache_len[r] + 1, and so on. `cache_len`: some request has exactly 256 cached tokens.
All inputs are finite; a program needn't handle non-finite values.
Results may differ from the reference program's by a relative error of at most 0.017.
Values may be sent and summed in bfloat16 or wider, within the bound.
No kernel may reach another device: no remote copies, remote signals or barrier semaphores. Data moves between devices by JAX's collectives and lax.ppermute only.
A program may use at most 128 MiB of HBM per device.

```python
import math
import jax
import jax.numpy as jnp
from jax import lax

MODEL_WIDTH = 8192
QUERY_HEADS = 64
KEY_VALUE_HEADS = 8
HEAD_SIZE = 128
SUB = 1024
RPO = 16
CACHE_SLOTS = 256
DECODE_STEPS = 4
REPLICAS = 8
OWNERS = 16
DECODE_REQUESTS = 256
PROMPT_TOKENS = 8192
CAP = 64


def anchor_keys(key):
    return jnp.clip(jax.random.normal(jax.random.fold_in(key, 200), (DECODE_REQUESTS, KEY_VALUE_HEADS, HEAD_SIZE), jnp.float32), -4.0, 4.0)


def request_layout(key):
    keys_all = jax.random.split(jax.random.fold_in(key, 300), 5)
    members = jax.random.permutation(keys_all[0], DECODE_REQUESTS).astype(jnp.int32)
    orders = jax.vmap(lambda single: jax.random.permutation(single, SUB))(jax.random.split(keys_all[1], REPLICAS))
    owner = (orders // CAP).astype(jnp.int32)
    shifts = jax.random.randint(keys_all[2], (REPLICAS, OWNERS), 0, RPO)
    picks = jax.random.randint(keys_all[3], (REPLICAS, SUB), 0, 2)
    shift_tok = jnp.take_along_axis(shifts, owner, axis=1)
    slots = owner * RPO + (shift_tok + picks) % RPO
    first_slot = jnp.argmax((members == 0).astype(jnp.int32)).astype(jnp.int32)
    first_owner = first_slot // RPO
    second_owner = (first_owner + 1) % OWNERS
    second_slot = second_owner * RPO
    slots = jnp.where(owner == first_owner, first_slot, jnp.where(owner == second_owner, second_slot, slots))
    span_req = members[slots.reshape(-1)].astype(jnp.int32)
    cache_len = jax.random.randint(keys_all[4], (DECODE_REQUESTS,), 2, CACHE_SLOTS + 1).astype(jnp.int32)
    cache_len = cache_len.at[0].set(CACHE_SLOTS).at[members[second_slot]].set(2).astype(jnp.int32)
    onehot = (span_req[:, None] == jnp.arange(DECODE_REQUESTS, dtype=jnp.int32)[None, :]).astype(jnp.int32)
    before = jnp.cumsum(onehot, axis=0) - onehot
    ranks = jnp.sum(before * onehot, axis=1)
    span_pos = (cache_len[span_req] + ranks).astype(jnp.int32)
    return (members, span_req, span_pos, cache_len)


def draw_members(key, part):
    return request_layout(key)[0]


def draw_span_req(key, part):
    return request_layout(key)[1]


def draw_span_pos(key, part):
    return request_layout(key)[2]


def draw_cache_len(key, part):
    return request_layout(key)[3]


def draw_kv_cache(key, part):
    start_offset = anchor_keys(key)
    key = jax.random.fold_in(key, 11)
    request_cache = jnp.clip(jax.random.normal(key, (DECODE_REQUESTS, CACHE_SLOTS, KEY_VALUE_HEADS, 2, HEAD_SIZE), jnp.float32), -4.0, 4.0)
    request_cache = request_cache.at[:, 0, :, 0, :].set(start_offset)
    return request_cache.astype(jnp.bfloat16)


def draw_queries(key, part):
    key = jax.random.fold_in(key, 12)
    attention_output = jnp.clip(jax.random.normal(key, (DECODE_STEPS, DECODE_REQUESTS, QUERY_HEADS, HEAD_SIZE), jnp.float32), -4.0, 4.0)
    return attention_output.astype(jnp.bfloat16)


def draw_span_x(key, part):
    key = jax.random.fold_in(key, 13)
    parts_keys = jax.random.split(key, 3)
    row_scale = jnp.exp(jax.random.uniform(parts_keys[0], (PROMPT_TOKENS, 1), jnp.float32, math.log(0.3), math.log(3.0)))
    col_scale = jnp.exp(jax.random.uniform(parts_keys[1], (1, MODEL_WIDTH), jnp.float32, math.log(0.3), math.log(3.0)))
    center = jnp.clip(jax.random.normal(parts_keys[2], (PROMPT_TOKENS, MODEL_WIDTH), jnp.float32), -4.0, 4.0)
    return (center * row_scale * col_scale).astype(jnp.bfloat16)


def level_of(key, extent, pieces, least, high):
    def one(dim, shards_of):
        draws = jax.random.uniform(jax.random.fold_in(jax.random.fold_in(key, 6), dim), (shards_of,), jnp.float32, least / len(pieces), high / len(pieces))
        return jnp.repeat(jnp.exp(draws), extent[dim] // shards_of).reshape((-1,) + (1,) * (len(extent) - dim - 1))

    factor_of = one(*pieces[0])
    for cut in pieces[1:]:
        factor_of = factor_of * one(*cut)
    return factor_of


def scatter_about(stream_key, dims, spread, bound, cuts=(), held_as=jnp.bfloat16):
    result = jax.random.normal(stream_key, dims, jnp.float32) * spread
    if len(cuts) > 0:
        result = level_of(stream_key, dims, cuts, -0.22, 0.18) * result
    return jnp.clip(result, min=-bound, max=bound).astype(held_as)


def setup_inputs(seed: int = 0) -> dict:
    seeds = jax.random.split(jax.random.key(seed), 13)
    return {
        "span_x": draw_span_x(jax.random.fold_in(seeds[12], 71), 0),
        "norm_gain": jnp.clip(1.0 + 0.18 * jax.random.normal(seeds[1], (MODEL_WIDTH,), jnp.float32), 0.099609375, 1.8984375).astype(jnp.bfloat16),
        "key_value_weight": scatter_about(seeds[2], (MODEL_WIDTH, KEY_VALUE_HEADS, 2, HEAD_SIZE), MODEL_WIDTH ** -0.5, 0.0625, ((1, 8), (2, 2))),
        "key_value_bias": scatter_about(seeds[3], (KEY_VALUE_HEADS, 2, HEAD_SIZE), 1.0, 4.0, ((0, 8), (1, 2))),
        "queries": draw_queries(jax.random.fold_in(seeds[12], 71), 0),
        "decode_key_value": scatter_about(seeds[5], (DECODE_STEPS, DECODE_REQUESTS, KEY_VALUE_HEADS, 2, HEAD_SIZE), 1.0, 4.0, ((1, 16), (2, 8))),
        "kv_cache": draw_kv_cache(jax.random.fold_in(seeds[12], 71), 0),
        "w_out": scatter_about(seeds[7], (QUERY_HEADS * HEAD_SIZE, MODEL_WIDTH), HEAD_SIZE ** -0.5, 0.5, ((0, 8), (1, 16))),
        "members": draw_members(jax.random.fold_in(seeds[12], 71), 0),
        "span_req": draw_span_req(jax.random.fold_in(seeds[12], 71), 0),
        "span_pos": draw_span_pos(jax.random.fold_in(seeds[12], 71), 0),
        "cache_len": draw_cache_len(jax.random.fold_in(seeds[12], 71), 0),
    }


EPSILON = 1e-06
THETA_BASE = 1000000.0
NEGATIVE = -1e+30

def rms_normed(span_x, norm_gain):
    as_float = span_x.astype(jnp.float32)
    square_mean = lax.optimization_barrier(jnp.mean(as_float * as_float, axis=-1, keepdims=True))
    return (as_float * lax.rsqrt(square_mean + EPSILON) * norm_gain.astype(jnp.float32)).astype(jnp.bfloat16)

def rotate_keys(values_in, positions):
    half_dim = values_in.shape[-1] // 2
    inv_freq = THETA_BASE ** (-jnp.arange(half_dim, dtype=jnp.float32) / half_dim)
    angles = positions.astype(jnp.float32)[:, None] * inv_freq[None, :]
    cosine = jnp.cos(angles)[:, None, :]
    sine_part = jnp.sin(angles)[:, None, :]
    first_half = values_in[..., :half_dim]
    second_half = values_in[..., half_dim:]
    return jnp.concatenate([first_half * cosine - second_half * sine_part, second_half * cosine + first_half * sine_part], axis=-1)

def reference(span_x, norm_gain, key_value_weight, key_value_bias, queries, decode_key_value, kv_cache, w_out, members, span_req, span_pos, cache_len):
    normalized_input = rms_normed(span_x, norm_gain)
    projected_rows = jnp.dot(normalized_input, key_value_weight.reshape(MODEL_WIDTH, KEY_VALUE_HEADS * 2 * HEAD_SIZE), preferred_element_type=jnp.float32)
    projected_rows = projected_rows + key_value_bias.reshape(KEY_VALUE_HEADS * 2 * HEAD_SIZE).astype(jnp.float32)
    projected_rows = projected_rows.reshape(PROMPT_TOKENS, KEY_VALUE_HEADS, 2, HEAD_SIZE)
    span_keys = lax.optimization_barrier(rotate_keys(projected_rows[:, :, 0, :], span_pos).astype(jnp.bfloat16)).astype(jnp.float32)
    span_values = lax.optimization_barrier(projected_rows[:, :, 1, :].astype(jnp.bfloat16)).astype(jnp.float32)
    scale = 1.0 / math.sqrt(HEAD_SIZE)
    heads_per_group = QUERY_HEADS // KEY_VALUE_HEADS
    step_ids = jnp.arange(DECODE_STEPS, dtype=jnp.int32)
    fresh_mask = step_ids[None, :] <= step_ids[:, None]

    def one_slot(decode_slot_index):
        request = members[decode_slot_index]
        grouped_queries = queries[:, decode_slot_index].astype(jnp.float32).reshape(DECODE_STEPS, KEY_VALUE_HEADS, heads_per_group, HEAD_SIZE)
        cache_keys = kv_cache[decode_slot_index, :, :, 0, :].astype(jnp.float32)
        cache_values = kv_cache[decode_slot_index, :, :, 1, :].astype(jnp.float32)
        fresh_keys = decode_key_value[:, decode_slot_index, :, 0, :].astype(jnp.float32)
        fresh_values = decode_key_value[:, decode_slot_index, :, 1, :].astype(jnp.float32)
        cache_mask = jnp.arange(CACHE_SLOTS, dtype=jnp.int32) < cache_len[request]
        span_mask = span_req == request
        cache_scores = jnp.einsum('jgmd,pgd->jgmp', grouped_queries, cache_keys) * scale
        span_scores = jnp.einsum('jgmd,tgd->jgmt', grouped_queries, span_keys) * scale
        fresh_scores = jnp.einsum('jgmd,igd->jgmi', grouped_queries, fresh_keys) * scale
        cache_scores = jnp.where(cache_mask[None, None, None, :], cache_scores, NEGATIVE)
        span_scores = jnp.where(span_mask[None, None, None, :], span_scores, NEGATIVE)
        fresh_scores = jnp.where(fresh_mask[:, None, None, :], fresh_scores, NEGATIVE)
        top = jnp.maximum(jnp.maximum(lax.optimization_barrier(jnp.max(cache_scores, axis=-1, keepdims=True)), lax.optimization_barrier(jnp.max(span_scores, axis=-1, keepdims=True))), lax.optimization_barrier(jnp.max(fresh_scores, axis=-1, keepdims=True)))
        cache_exp = jnp.where(cache_mask[None, None, None, :], jnp.exp(cache_scores - top), 0.0)
        span_exp = jnp.where(span_mask[None, None, None, :], jnp.exp(span_scores - top), 0.0)
        fresh_exp = jnp.where(fresh_mask[:, None, None, :], jnp.exp(fresh_scores - top), 0.0)
        total = lax.optimization_barrier(jnp.sum(cache_exp, axis=-1, keepdims=True)) + lax.optimization_barrier(jnp.sum(span_exp, axis=-1, keepdims=True)) + lax.optimization_barrier(jnp.sum(fresh_exp, axis=-1, keepdims=True))
        cache_weights = lax.optimization_barrier((cache_exp / total).astype(jnp.bfloat16)).astype(jnp.float32)
        span_weights = lax.optimization_barrier((span_exp / total).astype(jnp.bfloat16)).astype(jnp.float32)
        fresh_weights = lax.optimization_barrier((fresh_exp / total).astype(jnp.bfloat16)).astype(jnp.float32)
        mixed = jnp.einsum('jgmp,pgd->jgmd', cache_weights, cache_values)
        mixed = mixed + jnp.einsum('jgmt,tgd->jgmd', span_weights, span_values)
        mixed = mixed + jnp.einsum('jgmi,igd->jgmd', fresh_weights, fresh_values)
        return mixed.astype(jnp.bfloat16).reshape(DECODE_STEPS, QUERY_HEADS * HEAD_SIZE)
    attention = lax.map(one_slot, jnp.arange(DECODE_REQUESTS, dtype=jnp.int32))
    output = jnp.dot(attention.reshape(DECODE_REQUESTS * DECODE_STEPS, QUERY_HEADS * HEAD_SIZE), w_out, preferred_element_type=jnp.float32)
    return output.reshape(DECODE_REQUESTS, DECODE_STEPS, MODEL_WIDTH).astype(jnp.bfloat16)
```

```python
import functools
import math

import jax
import jax.numpy as jnp
import numpy as np
from jax import lax
from jax.experimental import pallas as pl
from jax.experimental.pallas import tpu as pltpu
from jax.sharding import PartitionSpec as P

EPSILON = 1e-06
THETA_BASE = 1000000.0
NEGATIVE = -1e30
F32 = jnp.float32
BF16 = jnp.bfloat16
MIB = 1024 * 1024


def nt_dot(a, b):
    return lax.dot_general(a, b, (((1,), (1,)), ((), ())), preferred_element_type=F32)


def nn_dot(a, b):
    return jnp.dot(a, b, preferred_element_type=F32)


def iota(shape, dim):
    return lax.broadcasted_iota(jnp.int32, shape, dim)


def as_mask(cond, dtype=BF16):
    return jnp.where(cond, 1.0, 0.0).astype(dtype)


def to_column(rows):
    eye = as_mask(iota((128, 128), 0) == iota((128, 128), 1))
    return nt_dot(eye, rows.astype(BF16))


def prefill_kernel(
    place,
    x_ref,
    gain_ref,
    weight_ref,
    bias_ref,
    freq_ref,
    request_ref,
    position_ref,
    member_ref,
    out_ref,
    acc_ref,
    square_ref,
    cos_ref,
    sin_ref,
    perm_ref,
    ids_ref,
    carry_ref,
    column_ref,
    poscol_ref,
):
    step = pl.program_id(0)
    steps = pl.num_programs(0)
    rows = x_ref.shape[0]
    width = x_ref.shape[1] * steps
    owners = out_ref.shape[0]
    capacity = rows // owners
    groups = rows // 128
    slots = member_ref.shape[0] * 128
    per_owner = slots // owners

    @pl.when(step == 0)
    def _():
        acc_ref[...] = jnp.zeros_like(acc_ref)
        square_ref[...] = jnp.zeros_like(square_ref)
        ids_ref[...] = jnp.zeros_like(ids_ref)
        carry_ref[...] = jnp.zeros_like(carry_ref)
        members = member_ref[...]
        filler = jnp.zeros((8 - members.shape[0], 128), jnp.int32)
        turned = to_column(jnp.concatenate([members, filler], axis=0).astype(F32))
        for part in range(slots // 128):
            column_ref[part * 128 : (part + 1) * 128, :] = jnp.broadcast_to(
                turned[:, part : part + 1], (128, 128)
            )
        positions = jnp.where(place[0] == 0, position_ref[...], 0)
        high = to_column((positions // 32).astype(F32))
        low = to_column((positions % 32).astype(F32))
        turned = high * 32.0 + low
        for part in range(groups):
            poscol_ref[part] = jnp.broadcast_to(turned[:, part : part + 1], (128, 128))

    lane = iota((128, 128), 1)
    angles = poscol_ref[step] * freq_ref[...]
    quarter = jnp.floor(angles * (2.0 / math.pi) + 0.5)
    rest = angles - quarter * 1.5703125
    rest = rest - quarter * 4.837512969970703125e-4
    rest = rest - quarter * 7.54978995489188216e-8
    square = rest * rest
    sine = rest + rest * square * (
        -1.6666654611e-1 + square * (8.3321608736e-3 + square * -1.9515295891e-4)
    )
    cosine = (
        1.0
        - 0.5 * square
        + square
        * square
        * (4.166664568298827e-2 + square * (-1.388731625493765e-3 + square * 2.443315711809948e-5))
    )
    turn = quarter.astype(jnp.int32) + jnp.where(lane < 64, 1, 0)
    table = jnp.where((turn & 1) == 1, cosine, sine)
    table = jnp.where((turn & 2) == 2, -table, table)
    swapped = pltpu.roll(table, 64, axis=1)
    cos_ref[step] = jnp.where(lane < 64, table, swapped)
    sin_ref[step] = jnp.where(lane < 64, -swapped, table)

    request_row = request_ref[pl.ds(step, 1), :].astype(F32)
    held = as_mask(column_ref[...] == request_row)
    pick_row = iota((32, slots), 0)
    pick_slot = iota((32, slots), 1)
    pick = jnp.where(pick_row == 16, pick_slot % per_owner, 0)
    pick = jnp.where((pick_row < 16) & (pick_slot // per_owner == pick_row), 1, pick)
    found = nn_dot(pick.astype(F32).astype(BF16), held)
    owner_hot = found[:16]
    slot_row = found[16:24]
    hot = owner_hot.astype(BF16)
    before = nn_dot(hot, as_mask(iota((128, 128), 0) < iota((128, 128), 1)))
    ranks = before + carry_ref[...] + (iota((16, 128), 0) * capacity).astype(F32)
    carry_ref[...] += nn_dot(hot, jnp.ones((128, 128), BF16))
    target = jnp.sum(owner_hot * ranks, axis=0, keepdims=True).astype(jnp.int32)
    chosen = as_mask(iota((rows, 128), 0) == target)
    perm_ref[step] = chosen
    ids_ref[...] += nt_dot(slot_row.astype(BF16), chosen)

    chunk = min(rows, 256)

    def project(index, _):
        start = pl.multiple_of(index * chunk, chunk)
        strips = []
        for strip in range(chunk // 16):
            block = x_ref[pl.ds(start + strip * 16, 16), :]
            strips.append(block * gain_ref[...])
            wide = block.astype(F32)
            wide = wide * wide
            total = wide[:, :128]
            for tile in range(1, wide.shape[1] // 128):
                total = total + wide[:, tile * 128 : (tile + 1) * 128]
            square_ref[pl.ds(start + strip * 16, 16), :] += total
        acc_ref[pl.ds(start, chunk), :] += nn_dot(
            jnp.concatenate(strips, axis=0), weight_ref[...]
        )
        return 0

    lax.fori_loop(0, rows // chunk, project, 0)

    @pl.when(step == steps - 1)
    def _():
        mean = jnp.sum(square_ref[...], axis=1, keepdims=True) / width
        scaled = acc_ref[...] * lax.rsqrt(mean + EPSILON) + bias_ref[...].astype(F32)
        cosines = cos_ref[...].reshape(rows, 128)
        sines = sin_ref[...].reshape(rows, 128)
        rotated = scaled * cosines + pltpu.roll(scaled, 64, axis=1) * sines
        rounded = rotated.astype(BF16)
        everything = jnp.concatenate([perm_ref[part] for part in range(groups)], axis=1)
        ordered = nn_dot(everything, rounded).astype(BF16)
        lanes = iota((16, 128), 1)
        for owner in range(owners):
            out_ref[owner, :capacity, :] = ordered[owner * capacity : (owner + 1) * capacity]
            pair = owner // 2
            ids = jnp.broadcast_to(ids_ref[0:1, pair * 128 : (pair + 1) * 128], (16, 128))
            other = pltpu.roll(ids, 64, axis=1)
            mine = (lanes < 64) if owner % 2 == 0 else (lanes >= 64)
            out_ref[owner, capacity:, :] = jnp.where(mine, ids, other).astype(BF16)


def prefill(place, span_x, norm_gain, weight, bias, span_req, span_pos, members, owners):
    rows, width = span_x.shape
    head_dim = weight.shape[1]
    groups = rows // 128
    tile = width // groups
    half = head_dim // 2
    freq = (THETA_BASE ** (-(np.arange(head_dim) % half) / half)).astype(np.float32)[None, :]
    whole = lambda *shape: pl.BlockSpec(shape, lambda k, place: (0,) * len(shape))
    mine = pl.BlockSpec((groups, 128), lambda k, place: (place[1], 0))
    return pl.pallas_call(
        prefill_kernel,
        out_shape=jax.ShapeDtypeStruct((owners, rows // owners + 16, head_dim), BF16),
        grid_spec=pltpu.PrefetchScalarGridSpec(
            num_scalar_prefetch=1,
            grid=(groups,),
            in_specs=[
                pl.BlockSpec((rows, tile), lambda k, place: (0, k)),
                pl.BlockSpec((1, tile), lambda k, place: (0, k)),
                pl.BlockSpec((tile, head_dim), lambda k, place: (k, 0)),
                whole(1, head_dim),
                whole(1, head_dim),
                mine,
                mine,
                whole(members.shape[0] // 128, 128),
            ],
            out_specs=whole(owners, rows // owners + 16, head_dim),
            scratch_shapes=[
                pltpu.VMEM((rows, 128), F32),
                pltpu.VMEM((rows, 128), F32),
                pltpu.VMEM((groups, 128, 128), F32),
                pltpu.VMEM((groups, 128, 128), F32),
                pltpu.VMEM((groups, rows, 128), BF16),
                pltpu.VMEM((8, rows), F32),
                pltpu.VMEM((16, 128), F32),
                pltpu.VMEM((members.shape[0], 128), F32),
                pltpu.VMEM((groups, 128, 128), F32),
            ],
        ),
        compiler_params=pltpu.CompilerParams(
            dimension_semantics=("arbitrary",), vmem_limit_bytes=48 * MIB
        ),
        cost_estimate=pl.CostEstimate(
            flops=2 * rows * width * head_dim, bytes_accessed=2 * rows * width, transcendentals=0
        ),
        name="prefill",
    )(
        place,
        span_x,
        norm_gain.reshape(1, width),
        weight,
        bias,
        jnp.asarray(freq),
        span_req.reshape(-1, 128),
        span_pos.reshape(-1, 128),
        members.reshape(-1, 128),
    )


def attention_kernel(
    lengths, query_ref, cache_ref, fresh_ref, row_ref, out_ref, q_ref, s_ref, p_ref, sum_ref, acc_ref
):
    steps, slots, heads, dim = query_ref.shape
    per_slot = steps * heads
    rows = slots * per_slot
    cached = cache_ref.shape[1]
    blocks = row_ref.shape[0] // 2
    capacity = row_ref.shape[1] - 16
    spanned = blocks * capacity
    newest = fresh_ref.shape[0]
    scale = 1.0 / math.sqrt(dim)
    for slot in range(slots):
        q_ref[slot * per_slot : (slot + 1) * per_slot, :] = jnp.concatenate(
            [query_ref[step, slot].astype(F32) for step in range(steps)], axis=0
        ).astype(BF16)
    column = iota((per_slot, cached), 1)
    for slot in range(slots):
        span = pl.ds(slot * per_slot, per_slot)
        scores = nt_dot(q_ref[span, :], cache_ref[slot]) * scale
        keep = ((column & 1) == 0) & (column < 2 * lengths[slot])
        s_ref[span, :cached] = jnp.where(keep, scores, NEGATIVE)
    keys = [row_ref[block, :capacity, :] for block in range(blocks)]
    values = [row_ref[blocks + block, :capacity, :] for block in range(blocks)]
    lane = iota((16, 128), 1)
    row_slot = iota((rows, 128), 0) // per_slot
    for pair in range(spanned // 128):
        scores = nt_dot(q_ref[...], jnp.concatenate(keys[2 * pair : 2 * pair + 2], axis=0)) * scale
        left = row_ref[2 * pair, capacity:, :].astype(F32)
        right = row_ref[2 * pair + 1, capacity:, :].astype(F32)
        ids = jnp.where(lane < 64, left, right)[0:1].astype(jnp.int32)
        s_ref[:, cached + pair * 128 : cached + (pair + 1) * 128] = jnp.where(
            row_slot == ids, scores, NEGATIVE
        )
    row = iota((rows, newest), 0)
    col = iota((rows, newest), 1)
    per_step = 2 * slots
    keep = (
        ((col & 1) == 0)
        & ((col % per_step) // 2 == row // per_slot)
        & (col // per_step <= (row % per_slot) // heads)
    )
    scores = nt_dot(q_ref[...], fresh_ref[...]) * scale
    s_ref[:, cached + spanned :] = jnp.where(keep, scores, NEGATIVE)
    for slot in range(slots):
        span = pl.ds(slot * per_slot, per_slot)
        scores = s_ref[span, :]
        top = jnp.max(scores, axis=1, keepdims=True)
        weights = jnp.exp(scores - top)
        sum_ref[span, :] = jnp.broadcast_to(jnp.sum(weights, axis=1, keepdims=True), (per_slot, dim))
        p_ref[span, :cached] = pltpu.roll(weights[:, :cached], 1, axis=1).astype(BF16)
        p_ref[span, cached : cached + spanned] = weights[:, cached : cached + spanned].astype(BF16)
        p_ref[span, cached + spanned :] = pltpu.roll(
            weights[:, cached + spanned :], 1, axis=1
        ).astype(BF16)
    acc_ref[...] = nn_dot(
        p_ref[:, cached : cached + spanned], jnp.concatenate(values, axis=0)
    ) + nn_dot(p_ref[:, cached + spanned :], fresh_ref[...])
    for slot in range(slots):
        span = pl.ds(slot * per_slot, per_slot)
        acc_ref[span, :] = (
            acc_ref[span, :] + nn_dot(p_ref[span, :cached], cache_ref[slot])
        ) / sum_ref[span, :]
    for head in range(heads):
        out_ref[head] = acc_ref[pl.ds(head, slots * steps, stride=heads), :].astype(BF16)


def attend(lengths, queries, cache, fresh, rows):
    steps, slots, heads, dim = queries.shape
    count = slots * steps * heads
    cached = cache.shape[1]
    spanned = (rows.shape[0] // 2) * (rows.shape[1] - 16)
    columns = cached + spanned + fresh.shape[0]
    vmem = pl.BlockSpec(memory_space=pltpu.VMEM)
    return pl.pallas_call(
        attention_kernel,
        out_shape=jax.ShapeDtypeStruct((heads, slots * steps, dim), BF16),
        in_specs=[pl.BlockSpec(memory_space=pltpu.SMEM)] + [vmem] * 4,
        out_specs=vmem,
        scratch_shapes=[
            pltpu.VMEM((count, dim), BF16),
            pltpu.VMEM((count, columns), F32),
            pltpu.VMEM((count, columns), BF16),
            pltpu.VMEM((count, dim), F32),
            pltpu.VMEM((count, dim), F32),
        ],
        compiler_params=pltpu.CompilerParams(vmem_limit_bytes=32 * MIB),
        name="attend",
    )(lengths, queries, cache, fresh, rows)


def body(
    span_x,
    norm_gain,
    key_value_weight,
    key_value_bias,
    queries,
    decode_key_value,
    kv_cache,
    w_out,
    members,
    span_req,
    span_pos,
    cache_len,
):
    n_role = lax.axis_size("role")
    n_batch = lax.axis_size("batch")
    owners = n_role * n_batch
    my_role = lax.axis_index("role")
    my_batch = lax.axis_index("batch")
    my_owner = my_role * n_batch + my_batch
    width = span_x.shape[1]
    head_dim = key_value_weight.shape[3]
    steps, slots, heads, _ = queries.shape
    place = jnp.stack([my_role, my_batch]).astype(jnp.int32)
    outgoing = prefill(
        place,
        span_x,
        norm_gain,
        key_value_weight.reshape(width, head_dim),
        key_value_bias.reshape(1, head_dim),
        span_req,
        span_pos,
        members,
        owners,
    )
    arrived = lax.all_to_all(outgoing, ("role", "batch"), 0, 0)
    my_members = lax.dynamic_slice_in_dim(members, my_owner * slots, slots)
    request_ids = jnp.arange(members.shape[0], dtype=jnp.int32)
    lengths = jnp.sum(
        jnp.where(my_members[:, None] == request_ids[None, :], cache_len[None, :], 0), axis=1
    )
    attention = attend(
        lengths,
        queries,
        kv_cache.reshape(slots, -1, head_dim),
        decode_key_value.reshape(-1, head_dim),
        arrived,
    )

    def shifted(k):
        pairs = []
        for i in range(n_batch):
            pairs.append((i, (((i // 4) ^ (k // 4)) * 4) + (i % 4 + k % 4) % 4))
        return pairs

    blocks = [attention]
    for k in range(1, n_batch):
        blocks.append(lax.ppermute(attention, "batch", shifted(k)))
    mine = jnp.stack(blocks)
    other = lax.ppermute(mine, "role", [(0, 1), (1, 0)])

    def rows_of(stack):
        return stack.transpose(0, 2, 1, 3).reshape(n_batch, slots * steps, heads * head_dim)

    def product(stack):
        return jnp.einsum("brc,cn->brn", rows_of(stack), w_out, preferred_element_type=F32).astype(
            BF16
        )

    sender = jnp.array(
        [[[s for s, d in shifted(k) if d == i][0] for k in range(n_batch)] for i in range(n_batch)],
        jnp.int32,
    )[my_batch]
    slot_of = jnp.sum(
        jnp.where(sender[None, :] == jnp.arange(n_batch)[:, None], jnp.arange(n_batch)[None, :], 0),
        axis=1,
    )
    first = jnp.where(my_role == 0, mine, other)
    second = jnp.where(my_role == 0, other, mine)
    partial = jnp.concatenate([product(first)[slot_of], product(second)[slot_of]], axis=0)
    n_tensor = lax.axis_size("tensor")
    partial = partial.reshape(n_tensor, -1, w_out.shape[1])
    summed = jnp.sum(lax.all_to_all(partial, "tensor", 0, 0).astype(F32), axis=0).astype(BF16)
    return summed.reshape(-1, steps, w_out.shape[1])


def solution(mesh):
    placed = (
        P("batch", None),
        P(),
        P(None, "tensor", "role", None),
        P("tensor", "role", None),
        P(None, ("role", "batch"), "tensor", None),
        P(None, ("role", "batch"), "tensor", None, None),
        P(("role", "batch"), None, "tensor", None, None),
        P("tensor", ("role", "batch")),
        P(),
        P(),
        P(),
        P(),
    )
    return jax.shard_map(
        body,
        mesh=mesh,
        in_specs=placed,
        out_specs=P("tensor", None, ("role", "batch")),
        check_vma=False,
    )
```

```python
import functools
import math

import jax
import jax.numpy as jnp
import numpy as np
from jax import lax
from jax.experimental import pallas as pl
from jax.experimental.pallas import tpu as pltpu
from jax.sharding import PartitionSpec as P

EPSILON = 1e-06
THETA_BASE = 1000000.0
NEGATIVE = -1e30
F32 = jnp.float32
BF16 = jnp.bfloat16
MIB = 1024 * 1024


def nt_dot(a, b):
    return lax.dot_general(a, b, (((1,), (1,)), ((), ())), preferred_element_type=F32)


def nn_dot(a, b):
    return jnp.dot(a, b, preferred_element_type=F32)


def iota(shape, dim):
    return lax.broadcasted_iota(jnp.int32, shape, dim)


def as_mask(cond, dtype=BF16):
    return jnp.where(cond, 1.0, 0.0).astype(dtype)


def to_column(rows):
    eye = as_mask(iota((128, 128), 0) == iota((128, 128), 1))
    return nt_dot(eye, rows.astype(BF16))


def prefill_kernel(
    place,
    x_hbm,
    weight_hbm,
    gain_hbm,
    bias_hbm,
    freq_hbm,
    request_hbm,
    position_hbm,
    member_hbm,
    out_ref,
    x_ref,
    weight_ref,
    gain_ref,
    bias_ref,
    freq_ref,
    request_ref,
    position_ref,
    member_ref,
    spread_ref,
    perm_ref,
    rounded_ref,
    x_sem,
    weight_sem,
    small_sem,
):
    rows, width = x_hbm.shape
    depth = x_ref.shape[0]
    owners = out_ref.shape[0]
    capacity = rows // owners
    groups = rows // 128
    slots = member_ref.shape[0] * 128
    per_owner = slots // owners

    block = pl.ds(pl.multiple_of(place[1] * groups, 8), groups)
    small = [
        pltpu.make_async_copy(source, target, small_sem.at[index])
        for index, (source, target) in enumerate(
            [
                (member_hbm, member_ref),
                (request_hbm.at[block, :], request_ref),
                (gain_hbm, gain_ref),
                (position_hbm.at[block, :], position_ref),
                (bias_hbm, bias_ref),
                (freq_hbm, freq_ref),
            ]
        )
    ]
    for copy in small:
        copy.start()
    whole_weight = pltpu.make_async_copy(weight_hbm, weight_ref, weight_sem)
    whole_weight.start()

    def load(group):
        return pltpu.make_async_copy(
            x_hbm.at[pl.ds(group * 128, 128), :], x_ref.at[group % depth], x_sem.at[group % depth]
        )

    for group in range(2):
        load(group).start()
    for copy in small:
        copy.wait()

    for tile in range(width // 128):
        spread_ref[:, tile * 128 : (tile + 1) * 128] = jnp.broadcast_to(
            gain_ref[tile : tile + 1, :], (16, 128)
        )

    members = member_ref[...]
    filler = jnp.zeros((8 - members.shape[0], 128), jnp.int32)
    turned = to_column(jnp.concatenate([members, filler], axis=0).astype(F32))
    member_column = jnp.concatenate(
        [
            jnp.broadcast_to(turned[:, part : part + 1], (128, 128))
            for part in range(slots // 128)
        ],
        axis=0,
    )
    pick_row = iota((32, slots), 0)
    pick_slot = iota((32, slots), 1)
    pick = jnp.where(pick_row == owners, pick_slot % per_owner, 0)
    pick = jnp.where((pick_row < owners) & (pick_slot // per_owner == pick_row), 1, pick)
    pick = pick.astype(F32).astype(BF16)
    earlier = as_mask(iota((128, 128), 0) < iota((128, 128), 1))
    ones = jnp.ones((128, 128), BF16)
    carry = (iota((owners, 128), 0) * capacity).astype(F32)
    ids = jnp.zeros((8, rows), F32)
    for group in range(groups):
        held = as_mask(member_column == request_ref[group : group + 1, :].astype(F32))
        found = nn_dot(pick, held)
        owner_hot = found[:owners]
        hot = owner_hot.astype(BF16)
        ranks = nn_dot(hot, earlier) + carry
        carry = carry + nn_dot(hot, ones)
        target = jnp.sum(owner_hot * ranks, axis=0, keepdims=True).astype(jnp.int32)
        chosen = as_mask(iota((rows, 128), 0) == target)
        perm_ref[group] = chosen
        ids = ids + nt_dot(found[owners : owners + 8].astype(BF16), chosen)

    positions = jnp.where(place[0] == 0, position_ref[...], 0)
    position_columns = 32.0 * to_column((positions >> 5).astype(F32)) + to_column(
        (positions & 31).astype(F32)
    )
    lane = iota((128, 128), 1)

    whole_weight.wait()
    for group in range(2, depth):
        load(group).start()
    piece = 1024
    for group in range(groups):
        load(group).wait()
        product = jnp.zeros((128, 128), F32)
        total = jnp.zeros((128, 128), F32)
        for start in range(0, width, piece):
            raw = x_ref[group % depth, :, start : start + piece]
            squares = raw * raw
            part = squares[:, :128]
            for tile in range(1, piece // 128):
                part = part + squares[:, tile * 128 : (tile + 1) * 128]
            total = total + part.astype(F32)
            gained = raw.reshape(8, 16, piece) * spread_ref[:, start : start + piece][None]
            product = product + nn_dot(
                gained.reshape(128, piece), weight_ref[start : start + piece, :]
            )
        if group + depth < groups:
            load(group + depth).start()
        mean = jnp.sum(total, axis=1, keepdims=True) / width
        scaled = product * lax.rsqrt(mean + EPSILON) + bias_ref[...].astype(F32)
        angles = position_columns[:, group : group + 1] * freq_ref[...]
        quarter = jnp.floor(angles * (2.0 / math.pi) + 0.5)
        rest = angles - quarter * 1.5703125
        rest = rest - quarter * 4.837512969970703125e-4
        rest = rest - quarter * 7.54978995489188216e-8
        square = rest * rest
        sine = rest + rest * square * (
            -1.6666654611e-1 + square * (8.3321608736e-3 + square * -1.9515295891e-4)
        )
        cosine = (
            1.0
            - 0.5 * square
            + square
            * square
            * (
                4.166664568298827e-2
                + square * (-1.388731625493765e-3 + square * 2.443315711809948e-5)
            )
        )
        turn = quarter.astype(jnp.int32) + jnp.where(lane < 64, 1, 0)
        table = jnp.where((turn & 1) == 1, cosine, sine)
        table = jnp.where((turn & 2) == 2, -table, table)
        swapped = pltpu.roll(table, 64, axis=1)
        cosines = jnp.where(lane < 64, table, swapped)
        sines = jnp.where(lane < 64, -swapped, table)
        rotated = scaled * cosines + pltpu.roll(scaled, 64, axis=1) * sines
        rounded_ref[group * 128 : (group + 1) * 128, :] = rotated.astype(BF16)

    everything = jnp.concatenate([perm_ref[group] for group in range(groups)], axis=1)
    ordered = nn_dot(everything, rounded_ref[...]).astype(BF16)
    lanes = iota((16, 128), 1)
    for owner in range(owners):
        out_ref[owner, :capacity, :] = ordered[owner * capacity : (owner + 1) * capacity]
        pair = owner // 2
        both = jnp.broadcast_to(ids[0:1, pair * 128 : (pair + 1) * 128], (16, 128))
        other = pltpu.roll(both, 64, axis=1)
        mine = (lanes < 64) if owner % 2 == 0 else (lanes >= 64)
        out_ref[owner, capacity:, :] = jnp.where(mine, both, other).astype(BF16)


def prefill(place, span_x, norm_gain, weight, bias, span_req, span_pos, members, owners):
    rows, width = span_x.shape
    head_dim = weight.shape[1]
    groups = rows // 128
    half = head_dim // 2
    depth = 4
    freq = (THETA_BASE ** (-(np.arange(head_dim) % half) / half)).astype(np.float32)[None, :]
    small = [
        norm_gain.reshape(-1, 128),
        bias,
        jnp.asarray(freq),
        span_req.reshape(-1, 128),
        span_pos.reshape(-1, 128),
        members.reshape(-1, 128),
    ]
    held = [small[0].shape, small[1].shape, small[2].shape]
    held += [(groups, 128), (groups, 128), small[5].shape]
    return pl.pallas_call(
        prefill_kernel,
        out_shape=jax.ShapeDtypeStruct((owners, rows // owners + 16, head_dim), BF16),
        in_specs=[pl.BlockSpec(memory_space=pltpu.SMEM)] + [pl.BlockSpec(memory_space=pl.ANY)] * 8,
        out_specs=pl.BlockSpec(memory_space=pltpu.VMEM),
        scratch_shapes=[
            pltpu.VMEM((depth, 128, width), BF16),
            pltpu.VMEM((width, head_dim), BF16),
        ]
        + [pltpu.VMEM(shape, array.dtype) for shape, array in zip(held, small)]
        + [
            pltpu.VMEM((16, width), BF16),
            pltpu.VMEM((groups, rows, 128), BF16),
            pltpu.VMEM((rows, head_dim), BF16),
            pltpu.SemaphoreType.DMA((depth,)),
            pltpu.SemaphoreType.DMA,
            pltpu.SemaphoreType.DMA((len(small),)),
        ],
        compiler_params=pltpu.CompilerParams(vmem_limit_bytes=60 * MIB),
        cost_estimate=pl.CostEstimate(
            flops=2 * rows * width * head_dim, bytes_accessed=2 * rows * width, transcendentals=0
        ),
        name="prefill",
    )(place, span_x, weight, *small)


def attention_kernel(
    place, members, cache_len, query_ref, cache_ref, fresh_ref, row_ref, out_ref, q_ref, s_ref, p_ref, sum_ref, acc_ref
):
    steps, slots, heads, dim = query_ref.shape
    per_slot = steps * heads
    rows = slots * per_slot
    cached = cache_ref.shape[1]
    blocks = row_ref.shape[0] // 2
    capacity = row_ref.shape[1] - 16
    spanned = blocks * capacity
    newest = fresh_ref.shape[0]
    scale = 1.0 / math.sqrt(dim)
    for slot in range(slots):
        q_ref[slot * per_slot : (slot + 1) * per_slot, :] = jnp.concatenate(
            [query_ref[step, slot].astype(F32) for step in range(steps)], axis=0
        ).astype(BF16)
    column = iota((per_slot, cached), 1)
    for slot in range(slots):
        span = pl.ds(slot * per_slot, per_slot)
        scores = nt_dot(q_ref[span, :], cache_ref[slot]) * scale
        owner = place[0] * (members.shape[0] // slots // 2) + place[1]
        length = cache_len[members[owner * slots + slot]]
        keep = ((column & 1) == 0) & (column < 2 * length)
        s_ref[span, :cached] = jnp.where(keep, scores, NEGATIVE)
    keys = [row_ref[block, :capacity, :] for block in range(blocks)]
    values = [row_ref[blocks + block, :capacity, :] for block in range(blocks)]
    lane = iota((16, 128), 1)
    row_slot = iota((rows, 128), 0) // per_slot
    for pair in range(spanned // 128):
        scores = nt_dot(q_ref[...], jnp.concatenate(keys[2 * pair : 2 * pair + 2], axis=0)) * scale
        left = row_ref[2 * pair, capacity:, :].astype(F32)
        right = row_ref[2 * pair + 1, capacity:, :].astype(F32)
        ids = jnp.where(lane < 64, left, right)[0:1].astype(jnp.int32)
        s_ref[:, cached + pair * 128 : cached + (pair + 1) * 128] = jnp.where(
            row_slot == ids, scores, NEGATIVE
        )
    row = iota((rows, newest), 0)
    col = iota((rows, newest), 1)
    per_step = 2 * slots
    keep = (
        ((col & 1) == 0)
        & ((col % per_step) // 2 == row // per_slot)
        & (col // per_step <= (row % per_slot) // heads)
    )
    scores = nt_dot(q_ref[...], fresh_ref[...]) * scale
    s_ref[:, cached + spanned :] = jnp.where(keep, scores, NEGATIVE)
    for slot in range(slots):
        span = pl.ds(slot * per_slot, per_slot)
        scores = s_ref[span, :]
        top = jnp.max(scores, axis=1, keepdims=True)
        weights = jnp.exp(scores - top)
        sum_ref[span, :] = jnp.broadcast_to(jnp.sum(weights, axis=1, keepdims=True), (per_slot, dim))
        p_ref[span, :cached] = pltpu.roll(weights[:, :cached], 1, axis=1).astype(BF16)
        p_ref[span, cached : cached + spanned] = weights[:, cached : cached + spanned].astype(BF16)
        p_ref[span, cached + spanned :] = pltpu.roll(
            weights[:, cached + spanned :], 1, axis=1
        ).astype(BF16)
    acc_ref[...] = nn_dot(
        p_ref[:, cached : cached + spanned], jnp.concatenate(values, axis=0)
    ) + nn_dot(p_ref[:, cached + spanned :], fresh_ref[...])
    for slot in range(slots):
        span = pl.ds(slot * per_slot, per_slot)
        acc_ref[span, :] = (
            acc_ref[span, :] + nn_dot(p_ref[span, :cached], cache_ref[slot])
        ) / sum_ref[span, :]
    for head in range(heads):
        out_ref[head] = acc_ref[pl.ds(head, slots * steps, stride=heads), :].astype(BF16)


def attend(place, members, cache_len, queries, cache, fresh, rows):
    steps, slots, heads, dim = queries.shape
    count = slots * steps * heads
    cached = cache.shape[1]
    spanned = (rows.shape[0] // 2) * (rows.shape[1] - 16)
    columns = cached + spanned + fresh.shape[0]
    vmem = pl.BlockSpec(memory_space=pltpu.VMEM)
    return pl.pallas_call(
        attention_kernel,
        out_shape=jax.ShapeDtypeStruct((heads, slots * steps, dim), BF16),
        in_specs=[pl.BlockSpec(memory_space=pltpu.SMEM)] * 3 + [vmem] * 4,
        out_specs=vmem,
        scratch_shapes=[
            pltpu.VMEM((count, dim), BF16),
            pltpu.VMEM((count, columns), F32),
            pltpu.VMEM((count, columns), BF16),
            pltpu.VMEM((count, dim), F32),
            pltpu.VMEM((count, dim), F32),
        ],
        compiler_params=pltpu.CompilerParams(vmem_limit_bytes=32 * MIB),
        name="attend",
    )(place, members, cache_len, queries, cache, fresh, rows)


AXES = ("role", "batch", "tensor")


def gather_round(k):
    pairs = []
    for source in range(128):
        role, batch, tensor = source // 64, source // 8 % 8, source % 8
        x_lo, z, y, x_hi = batch // 4, batch % 4, tensor // 2, tensor % 2
        to_x_lo = x_lo ^ (k >> 2)
        to_z = 2 * (x_hi ^ (k >> 1 & 1)) + ((z & 1) ^ (k & 1))
        pairs.append((source, role * 64 + (to_x_lo * 4 + to_z) * 8 + y * 2 + z // 2))
    return pairs


def project_kernel(place, mine_ref, other_ref, own_ref, partner_ref, *rest):
    outs, staged = rest[:4], rest[4]
    role, batch, tensor = place[0], place[1], place[2]
    x_lo, z_top, z_low = batch >> 2, (batch >> 1) & 1, batch & 1
    y, x_hi = tensor >> 1, tensor & 1
    heads, rows, _ = mine_ref.shape[1:]

    def wide(ref, top):
        blocks = []
        for k in range(8):
            if (k >> 1 & 1) == top:
                blocks.append(
                    jnp.concatenate([ref[k, head] for head in range(heads)], axis=1)
                )
        return jnp.concatenate(blocks, axis=0)

    def work(first, second):
        for step, ref in enumerate((mine_ref, other_ref)):
            product = nn_dot(wide(ref, 0), first[...]) + nn_dot(wide(ref, 1), second[...])
            for index in range(4):
                row_y = 2 * (role ^ step) + (x_lo ^ (index >> 1))
                start = pl.multiple_of((z_low ^ (index & 1)) * rows, rows)
                staged[row_y ^ y, pl.ds(start, rows), :] = product[
                    index * rows : (index + 1) * rows
                ].astype(BF16)

    @pl.when(z_top == x_hi)
    def _():
        work(own_ref, partner_ref)

    @pl.when(z_top != x_hi)
    def _():
        work(partner_ref, own_ref)

    for turn in range(4):
        outs[turn][...] = staged[turn]


def project_out(place, mine, other, own, partner):
    _, heads, rows, _ = mine.shape
    columns = own.shape[1]
    vmem = pl.BlockSpec(memory_space=pltpu.VMEM)
    return pl.pallas_call(
        project_kernel,
        out_shape=[jax.ShapeDtypeStruct((2 * rows, columns), BF16)] * 4,
        in_specs=[pl.BlockSpec(memory_space=pltpu.SMEM)] + [vmem] * 4,
        out_specs=[vmem] * 4,
        scratch_shapes=[pltpu.VMEM((4, 2 * rows, columns), BF16)],
        compiler_params=pltpu.CompilerParams(vmem_limit_bytes=32 * MIB),
        name="project_out",
    )(place, mine, other, own, partner)


def body(
    span_x,
    norm_gain,
    key_value_weight,
    key_value_bias,
    queries,
    decode_key_value,
    kv_cache,
    w_out,
    members,
    span_req,
    span_pos,
    cache_len,
):
    n_role = lax.axis_size("role")
    n_batch = lax.axis_size("batch")
    owners = n_role * n_batch
    my_role = lax.axis_index("role")
    my_batch = lax.axis_index("batch")
    width = span_x.shape[1]
    head_dim = key_value_weight.shape[3]
    steps, slots, heads, _ = queries.shape
    place = jnp.stack([my_role, my_batch, lax.axis_index("tensor")]).astype(jnp.int32)
    partner = lax.ppermute(w_out, "tensor", [(t, t ^ 1) for t in range(8)])
    outgoing = prefill(
        place,
        span_x,
        norm_gain,
        key_value_weight.reshape(width, head_dim),
        key_value_bias.reshape(1, head_dim),
        span_req,
        span_pos,
        members,
        owners,
    )
    arrived = lax.all_to_all(outgoing, ("role", "batch"), 0, 0)
    attention = attend(
        place,
        members,
        cache_len,
        queries,
        kv_cache.reshape(slots, -1, head_dim),
        decode_key_value.reshape(-1, head_dim),
        arrived,
    )

    gathered = jnp.stack([lax.ppermute(attention, AXES, gather_round(k)) for k in range(8)])
    other = lax.ppermute(gathered, "role", [(0, 1), (1, 0)])
    parts = project_out(place, gathered, other, w_out, partner)
    total = parts[0].astype(F32)
    for turn in range(1, 4):
        total = total + lax.ppermute(
            parts[turn], "tensor", [(t, t ^ (2 * turn)) for t in range(8)]
        ).astype(F32)
    return total.astype(BF16).reshape(-1, steps, w_out.shape[1])


def solution(mesh):
    placed = (
        P("batch", None),
        P(),
        P(None, "tensor", "role", None),
        P("tensor", "role", None),
        P(None, ("role", "batch"), "tensor", None),
        P(None, ("role", "batch"), "tensor", None, None),
        P(("role", "batch"), None, "tensor", None, None),
        P("tensor", ("role", "batch")),
        P(),
        P(),
        P(),
        P(),
    )
    return jax.shard_map(
        body,
        mesh=mesh,
        in_specs=placed,
        out_specs=P("tensor", None, ("role", "batch")),
        check_vma=False,
    )
```

```python
import functools
import math

import jax
import jax.numpy as jnp
import numpy as np
from jax import lax
from jax.experimental import pallas as pl
from jax.experimental.pallas import tpu as pltpu
from jax.sharding import PartitionSpec as P

EPSILON = 1e-06
THETA_BASE = 1000000.0
NEGATIVE = -1e30
F32 = jnp.float32
BF16 = jnp.bfloat16
MIB = 1024 * 1024


def nt_dot(a, b):
    return lax.dot_general(a, b, (((1,), (1,)), ((), ())), preferred_element_type=F32)


def nn_dot(a, b):
    return jnp.dot(a, b, preferred_element_type=F32)


def iota(shape, dim):
    return lax.broadcasted_iota(jnp.int32, shape, dim)


def as_mask(cond, dtype=BF16):
    return jnp.where(cond, 1.0, 0.0).astype(dtype)


def to_column(rows):
    eye = as_mask(iota((128, 128), 0) == iota((128, 128), 1))
    return nt_dot(eye, rows.astype(BF16))


def prefill_kernel(
    place,
    x_hbm,
    weight_hbm,
    gain_hbm,
    bias_hbm,
    freq_hbm,
    request_hbm,
    position_hbm,
    member_hbm,
    out_ref,
    x_ref,
    weight_ref,
    gain_ref,
    bias_ref,
    freq_ref,
    request_ref,
    position_ref,
    member_ref,
    spread_ref,
    perm_ref,
    rounded_ref,
    x_sem,
    weight_sem,
    small_sem,
):
    rows, width = x_hbm.shape
    depth = x_ref.shape[0]
    owners = out_ref.shape[0]
    capacity = rows // owners
    groups = rows // 128
    slots = member_ref.shape[0] * 128
    per_owner = slots // owners

    block = pl.ds(pl.multiple_of(place[1] * groups, 8), groups)
    small = [
        pltpu.make_async_copy(source, target, small_sem.at[index])
        for index, (source, target) in enumerate(
            [
                (member_hbm, member_ref),
                (request_hbm.at[block, :], request_ref),
                (gain_hbm, gain_ref),
                (position_hbm.at[block, :], position_ref),
                (bias_hbm, bias_ref),
                (freq_hbm, freq_ref),
            ]
        )
    ]
    for copy in small:
        copy.start()
    whole_weight = pltpu.make_async_copy(weight_hbm, weight_ref, weight_sem)
    whole_weight.start()

    def load(group):
        return pltpu.make_async_copy(
            x_hbm.at[pl.ds(group * 128, 128), :], x_ref.at[group % depth], x_sem.at[group % depth]
        )

    for group in range(2):
        load(group).start()
    for copy in small:
        copy.wait()

    for tile in range(width // 128):
        spread_ref[:, tile * 128 : (tile + 1) * 128] = jnp.broadcast_to(
            gain_ref[tile : tile + 1, :], (16, 128)
        )

    members = member_ref[...]
    filler = jnp.zeros((8 - members.shape[0], 128), jnp.int32)
    turned = to_column(jnp.concatenate([members, filler], axis=0).astype(F32))
    member_column = jnp.concatenate(
        [
            jnp.broadcast_to(turned[:, part : part + 1], (128, 128))
            for part in range(slots // 128)
        ],
        axis=0,
    )
    pick_row = iota((32, slots), 0)
    pick_slot = iota((32, slots), 1)
    pick = jnp.where(pick_row == owners, pick_slot % per_owner, 0)
    pick = jnp.where((pick_row < owners) & (pick_slot // per_owner == pick_row), 1, pick)
    pick = pick.astype(F32).astype(BF16)
    earlier = as_mask(iota((128, 128), 0) < iota((128, 128), 1))
    ones = jnp.ones((128, 128), BF16)
    carry = (iota((owners, 128), 0) * capacity).astype(F32)
    ids = jnp.zeros((8, rows), F32)
    for group in range(groups):
        held = as_mask(member_column == request_ref[group : group + 1, :].astype(F32))
        found = nn_dot(pick, held)
        owner_hot = found[:owners]
        hot = owner_hot.astype(BF16)
        ranks = nn_dot(hot, earlier) + carry
        carry = carry + nn_dot(hot, ones)
        target = jnp.sum(owner_hot * ranks, axis=0, keepdims=True).astype(jnp.int32)
        chosen = as_mask(iota((rows, 128), 0) == target)
        perm_ref[group] = chosen
        ids = ids + nt_dot(found[owners : owners + 8].astype(BF16), chosen)

    positions = jnp.where(place[0] == 0, position_ref[...], 0)
    position_columns = 32.0 * to_column((positions >> 5).astype(F32)) + to_column(
        (positions & 31).astype(F32)
    )
    lane = iota((128, 128), 1)

    whole_weight.wait()
    for group in range(2, depth):
        load(group).start()
    piece = 1024
    for group in range(groups):
        load(group).wait()
        product = jnp.zeros((128, 128), F32)
        total = jnp.zeros((128, 128), F32)
        for start in range(0, width, piece):
            raw = x_ref[group % depth, :, start : start + piece]
            squares = raw * raw
            part = squares[:, :128]
            for tile in range(1, piece // 128):
                part = part + squares[:, tile * 128 : (tile + 1) * 128]
            total = total + part.astype(F32)
            gained = raw.reshape(8, 16, piece) * spread_ref[:, start : start + piece][None]
            product = product + nn_dot(
                gained.reshape(128, piece), weight_ref[start : start + piece, :]
            )
        if group + depth < groups:
            load(group + depth).start()
        mean = jnp.sum(total, axis=1, keepdims=True) / width
        scaled = product * lax.rsqrt(mean + EPSILON) + bias_ref[...].astype(F32)
        angles = position_columns[:, group : group + 1] * freq_ref[...]
        quarter = jnp.floor(angles * (2.0 / math.pi) + 0.5)
        rest = angles - quarter * 1.5703125
        rest = rest - quarter * 4.837512969970703125e-4
        rest = rest - quarter * 7.54978995489188216e-8
        square = rest * rest
        sine = rest + rest * square * (
            -1.6666654611e-1 + square * (8.3321608736e-3 + square * -1.9515295891e-4)
        )
        cosine = (
            1.0
            - 0.5 * square
            + square
            * square
            * (
                4.166664568298827e-2
                + square * (-1.388731625493765e-3 + square * 2.443315711809948e-5)
            )
        )
        turn = quarter.astype(jnp.int32) + jnp.where(lane < 64, 1, 0)
        table = jnp.where((turn & 1) == 1, cosine, sine)
        table = jnp.where((turn & 2) == 2, -table, table)
        swapped = pltpu.roll(table, 64, axis=1)
        cosines = jnp.where(lane < 64, table, swapped)
        sines = jnp.where(lane < 64, -swapped, table)
        rotated = scaled * cosines + pltpu.roll(scaled, 64, axis=1) * sines
        rounded_ref[group * 128 : (group + 1) * 128, :] = rotated.astype(BF16)

    everything = jnp.concatenate([perm_ref[group] for group in range(groups)], axis=1)
    ordered = nn_dot(everything, rounded_ref[...]).astype(BF16)
    lanes = iota((16, 128), 1)
    for owner in range(owners):
        out_ref[owner, :capacity, :] = ordered[owner * capacity : (owner + 1) * capacity]
        pair = owner // 2
        both = jnp.broadcast_to(ids[0:1, pair * 128 : (pair + 1) * 128], (16, 128))
        other = pltpu.roll(both, 64, axis=1)
        mine = (lanes < 64) if owner % 2 == 0 else (lanes >= 64)
        out_ref[owner, capacity:, :] = jnp.where(mine, both, other).astype(BF16)


def prefill(place, span_x, norm_gain, weight, bias, span_req, span_pos, members, owners):
    rows, width = span_x.shape
    head_dim = weight.shape[1]
    groups = rows // 128
    half = head_dim // 2
    depth = 4
    freq = (THETA_BASE ** (-(np.arange(head_dim) % half) / half)).astype(np.float32)[None, :]
    small = [
        norm_gain.reshape(-1, 128),
        bias,
        jnp.asarray(freq),
        span_req.reshape(-1, 128),
        span_pos.reshape(-1, 128),
        members.reshape(-1, 128),
    ]
    held = [small[0].shape, small[1].shape, small[2].shape]
    held += [(groups, 128), (groups, 128), small[5].shape]
    return pl.pallas_call(
        prefill_kernel,
        out_shape=jax.ShapeDtypeStruct((owners, rows // owners + 16, head_dim), BF16),
        in_specs=[pl.BlockSpec(memory_space=pltpu.SMEM)] + [pl.BlockSpec(memory_space=pl.ANY)] * 8,
        out_specs=pl.BlockSpec(memory_space=pltpu.VMEM),
        scratch_shapes=[
            pltpu.VMEM((depth, 128, width), BF16),
            pltpu.VMEM((width, head_dim), BF16),
        ]
        + [pltpu.VMEM(shape, array.dtype) for shape, array in zip(held, small)]
        + [
            pltpu.VMEM((16, width), BF16),
            pltpu.VMEM((groups, rows, 128), BF16),
            pltpu.VMEM((rows, head_dim), BF16),
            pltpu.SemaphoreType.DMA((depth,)),
            pltpu.SemaphoreType.DMA,
            pltpu.SemaphoreType.DMA((len(small),)),
        ],
        compiler_params=pltpu.CompilerParams(vmem_limit_bytes=60 * MIB),
        cost_estimate=pl.CostEstimate(
            flops=2 * rows * width * head_dim, bytes_accessed=2 * rows * width, transcendentals=0
        ),
        name="prefill",
    )(place, span_x, weight, *small)


def attention_kernel(
    place, members, cache_len, query_ref, cache_ref, fresh_ref, row_ref, out_ref, q_ref, s_ref, p_ref, sum_ref, acc_ref
):
    steps, slots, heads, dim = query_ref.shape
    per_slot = steps * heads
    rows = slots * per_slot
    cached = cache_ref.shape[1]
    blocks = row_ref.shape[0] // 2
    capacity = row_ref.shape[1] - 16
    spanned = blocks * capacity
    newest = fresh_ref.shape[0]
    scale = 1.0 / math.sqrt(dim)
    for slot in range(slots):
        q_ref[slot * per_slot : (slot + 1) * per_slot, :] = jnp.concatenate(
            [query_ref[step, slot].astype(F32) for step in range(steps)], axis=0
        ).astype(BF16)
    column = iota((per_slot, cached), 1)
    for slot in range(slots):
        span = pl.ds(slot * per_slot, per_slot)
        scores = nt_dot(q_ref[span, :], cache_ref[slot]) * scale
        owner = place[0] * (members.shape[0] // slots // 2) + place[1]
        length = cache_len[members[owner * slots + slot]]
        keep = ((column & 1) == 0) & (column < 2 * length)
        s_ref[span, :cached] = jnp.where(keep, scores, NEGATIVE)
    keys = [row_ref[block, :capacity, :] for block in range(blocks)]
    values = [row_ref[blocks + block, :capacity, :] for block in range(blocks)]
    lane = iota((16, 128), 1)
    row_slot = iota((rows, 128), 0) // per_slot
    for pair in range(spanned // 128):
        scores = nt_dot(q_ref[...], jnp.concatenate(keys[2 * pair : 2 * pair + 2], axis=0)) * scale
        left = row_ref[2 * pair, capacity:, :].astype(F32)
        right = row_ref[2 * pair + 1, capacity:, :].astype(F32)
        ids = jnp.where(lane < 64, left, right)[0:1].astype(jnp.int32)
        s_ref[:, cached + pair * 128 : cached + (pair + 1) * 128] = jnp.where(
            row_slot == ids, scores, NEGATIVE
        )
    row = iota((rows, newest), 0)
    col = iota((rows, newest), 1)
    per_step = 2 * slots
    keep = (
        ((col & 1) == 0)
        & ((col % per_step) // 2 == row // per_slot)
        & (col // per_step <= (row % per_slot) // heads)
    )
    scores = nt_dot(q_ref[...], fresh_ref[...]) * scale
    s_ref[:, cached + spanned :] = jnp.where(keep, scores, NEGATIVE)
    for slot in range(slots):
        span = pl.ds(slot * per_slot, per_slot)
        scores = s_ref[span, :]
        top = jnp.max(scores, axis=1, keepdims=True)
        weights = jnp.exp(scores - top)
        sum_ref[span, :] = jnp.broadcast_to(jnp.sum(weights, axis=1, keepdims=True), (per_slot, dim))
        p_ref[span, :cached] = pltpu.roll(weights[:, :cached], 1, axis=1).astype(BF16)
        p_ref[span, cached : cached + spanned] = weights[:, cached : cached + spanned].astype(BF16)
        p_ref[span, cached + spanned :] = pltpu.roll(
            weights[:, cached + spanned :], 1, axis=1
        ).astype(BF16)
    acc_ref[...] = nn_dot(
        p_ref[:, cached : cached + spanned], jnp.concatenate(values, axis=0)
    ) + nn_dot(p_ref[:, cached + spanned :], fresh_ref[...])
    for slot in range(slots):
        span = pl.ds(slot * per_slot, per_slot)
        acc_ref[span, :] = (
            acc_ref[span, :] + nn_dot(p_ref[span, :cached], cache_ref[slot])
        ) / sum_ref[span, :]
    for head in range(heads):
        out_ref[head] = acc_ref[pl.ds(head, slots * steps, stride=heads), :].astype(BF16)


def attend(place, members, cache_len, queries, cache, fresh, rows):
    steps, slots, heads, dim = queries.shape
    count = slots * steps * heads
    cached = cache.shape[1]
    spanned = (rows.shape[0] // 2) * (rows.shape[1] - 16)
    columns = cached + spanned + fresh.shape[0]
    vmem = pl.BlockSpec(memory_space=pltpu.VMEM)
    return pl.pallas_call(
        attention_kernel,
        out_shape=jax.ShapeDtypeStruct((heads, slots * steps, dim), BF16),
        in_specs=[pl.BlockSpec(memory_space=pltpu.SMEM)] * 3 + [vmem] * 4,
        out_specs=vmem,
        scratch_shapes=[
            pltpu.VMEM((count, dim), BF16),
            pltpu.VMEM((count, columns), F32),
            pltpu.VMEM((count, columns), BF16),
            pltpu.VMEM((count, dim), F32),
            pltpu.VMEM((count, dim), F32),
        ],
        compiler_params=pltpu.CompilerParams(vmem_limit_bytes=32 * MIB),
        name="attend",
    )(place, members, cache_len, queries, cache, fresh, rows)


AXES = ("role", "batch", "tensor")


def places(device):
    batch, tensor = device // 8 % 8, device % 8
    return device // 64, batch // 4, batch % 4, tensor // 2, tensor % 2


def moves(target):
    pairs = []
    for source in range(128):
        role, x_lo, z, y, x_hi = target(*places(source))
        pairs.append((source, role * 64 + (x_lo * 4 + z) * 8 + y * 2 + x_hi))
    return pairs


def sum_round(k):
    return moves(
        lambda role, x_lo, z, y, x_hi: (
            role,
            (y & 1) ^ (k & 1),
            z,
            2 * ((y >> 1) ^ (k >> 2)) + x_lo,
            x_hi ^ (k >> 1 & 1),
        )
    )


def project_kernel(place, mine_ref, other_ref, own_ref, x_ref, *rest):
    outs, staged = rest[:-1], rest[-1]
    role, batch, tensor = place[0], place[1], place[2]
    x_lo, z_top, z_low = batch >> 2, (batch >> 1) & 1, batch & 1
    y, x_hi = tensor >> 1, tensor & 1
    blocks, heads, rows, _ = mine_ref.shape
    for step, ref in enumerate((mine_ref, other_ref)):
        left = jnp.concatenate(
            [
                jnp.concatenate([ref[block, head] for head in range(heads)], axis=1)
                for block in range(blocks)
            ],
            axis=0,
        )
        for turn, weight in enumerate((own_ref, x_ref)):
            product = nn_dot(left, weight[...]).astype(BF16)
            for block in range(blocks):
                slot = 4 * (role ^ step ^ (y >> 1))
                slot += 2 * (z_top ^ (block >> 1) ^ x_hi) + (x_lo ^ turn ^ (y & 1))
                start = pl.multiple_of((z_low ^ (block & 1)) * rows, rows)
                staged[slot, pl.ds(start, rows), :] = product[block * rows : (block + 1) * rows]
    for turn, out in enumerate(outs):
        out[...] = staged[turn]


def project_out(place, mine, other, *weights):
    _, heads, rows, _ = mine.shape
    columns = weights[0].shape[1]
    vmem = pl.BlockSpec(memory_space=pltpu.VMEM)
    return pl.pallas_call(
        project_kernel,
        out_shape=[jax.ShapeDtypeStruct((2 * rows, columns), BF16)] * 8,
        in_specs=[pl.BlockSpec(memory_space=pltpu.SMEM)] + [vmem] * 4,
        out_specs=[vmem] * 8,
        scratch_shapes=[pltpu.VMEM((8, 2 * rows, columns), BF16)],
        compiler_params=pltpu.CompilerParams(vmem_limit_bytes=32 * MIB),
        name="project_out",
    )(place, mine, other, *weights)


def body(
    span_x,
    norm_gain,
    key_value_weight,
    key_value_bias,
    queries,
    decode_key_value,
    kv_cache,
    w_out,
    members,
    span_req,
    span_pos,
    cache_len,
):
    n_role = lax.axis_size("role")
    n_batch = lax.axis_size("batch")
    owners = n_role * n_batch
    my_role = lax.axis_index("role")
    my_batch = lax.axis_index("batch")
    width = span_x.shape[1]
    head_dim = key_value_weight.shape[3]
    steps, slots, heads, _ = queries.shape
    place = jnp.stack([my_role, my_batch, lax.axis_index("tensor")]).astype(jnp.int32)
    beside = lax.ppermute(w_out, "batch", [(b, b ^ 4) for b in range(8)])
    outgoing = prefill(
        place,
        span_x,
        norm_gain,
        key_value_weight.reshape(width, head_dim),
        key_value_bias.reshape(1, head_dim),
        span_req,
        span_pos,
        members,
        owners,
    )
    arrived = lax.all_to_all(outgoing, ("role", "batch"), 0, 0)
    arrived, beside = lax.optimization_barrier((arrived, beside))
    attention = attend(
        place,
        members,
        cache_len,
        queries,
        kv_cache.reshape(slots, -1, head_dim),
        decode_key_value.reshape(-1, head_dim),
        arrived,
    )

    gathered = jnp.stack(
        [attention]
        + [lax.ppermute(attention, "batch", [(b, b ^ k) for b in range(8)]) for k in range(1, 4)]
    )
    other = lax.ppermute(gathered, "role", [(0, 1), (1, 0)])
    parts = project_out(place, gathered, other, w_out, beside)
    total = sum(lax.ppermute(parts[k], AXES, sum_round(k)).astype(F32) for k in range(8))
    return total.astype(BF16).reshape(-1, steps, w_out.shape[1])


def solution(mesh):
    placed = (
        P("batch", None),
        P(),
        P(None, "tensor", "role", None),
        P("tensor", "role", None),
        P(None, ("role", "batch"), "tensor", None),
        P(None, ("role", "batch"), "tensor", None, None),
        P(("role", "batch"), None, "tensor", None, None),
        P("tensor", ("role", "batch")),
        P(),
        P(),
        P(),
        P(),
    )
    return jax.shard_map(
        body,
        mesh=mesh,
        in_specs=placed,
        out_specs=P("tensor", None, ("role", "batch")),
        check_vma=False,
    )
```

```python
import functools
import math

import jax
import jax.numpy as jnp
import numpy as np
from jax import lax
from jax.experimental import pallas as pl
from jax.experimental.pallas import tpu as pltpu
from jax.sharding import PartitionSpec as P

EPSILON = 1e-06
THETA_BASE = 1000000.0
NEGATIVE = -1e30
F32 = jnp.float32
BF16 = jnp.bfloat16
MIB = 1024 * 1024


def nt_dot(a, b):
    return lax.dot_general(a, b, (((1,), (1,)), ((), ())), preferred_element_type=F32)


def nn_dot(a, b):
    return jnp.dot(a, b, preferred_element_type=F32)


def iota(shape, dim):
    return lax.broadcasted_iota(jnp.int32, shape, dim)


def as_mask(cond, dtype=BF16):
    return jnp.where(cond, 1.0, 0.0).astype(dtype)


def to_column(rows):
    eye = as_mask(iota((128, 128), 0) == iota((128, 128), 1))
    return nt_dot(eye, rows.astype(BF16))


def prefill_kernel(
    x_hbm,
    weight_hbm,
    gain_hbm,
    bias_hbm,
    freq_hbm,
    request_hbm,
    position_hbm,
    member_hbm,
    out_ref,
    x_ref,
    weight_ref,
    gain_ref,
    bias_ref,
    freq_ref,
    request_ref,
    position_ref,
    member_ref,
    spread_ref,
    perm_ref,
    rounded_ref,
    x_sem,
    weight_sem,
    small_sem,
):
    role, batch = lax.axis_index("role"), lax.axis_index("batch")
    rows, width = x_hbm.shape
    depth = x_ref.shape[0]
    owners = out_ref.shape[0]
    capacity = rows // owners
    groups = rows // 128
    slots = member_ref.shape[0] * 128
    per_owner = slots // owners

    block = pl.ds(pl.multiple_of(batch * groups, 8), groups)
    small = [
        pltpu.make_async_copy(source, target, small_sem.at[index])
        for index, (source, target) in enumerate(
            [
                (member_hbm, member_ref),
                (request_hbm.at[block, :], request_ref),
                (gain_hbm, gain_ref),
                (position_hbm.at[block, :], position_ref),
                (bias_hbm, bias_ref),
                (freq_hbm, freq_ref),
            ]
        )
    ]
    for copy in small:
        copy.start()
    whole_weight = pltpu.make_async_copy(weight_hbm, weight_ref, weight_sem)
    whole_weight.start()

    def load(group):
        return pltpu.make_async_copy(
            x_hbm.at[pl.ds(group * 128, 128), :], x_ref.at[group % depth], x_sem.at[group % depth]
        )

    for group in range(2):
        load(group).start()
    for copy in small:
        copy.wait()

    for tile in range(width // 128):
        spread_ref[:, tile * 128 : (tile + 1) * 128] = jnp.broadcast_to(
            gain_ref[tile : tile + 1, :], (16, 128)
        )

    members = member_ref[...]
    filler = jnp.zeros((8 - members.shape[0], 128), jnp.int32)
    turned = to_column(jnp.concatenate([members, filler], axis=0).astype(F32))
    requests = request_ref[...].astype(F32)
    held = jnp.concatenate(
        [
            jnp.concatenate(
                [
                    as_mask(turned[:, part : part + 1] == requests[group : group + 1, :])
                    for group in range(groups)
                ],
                axis=1,
            )
            for part in range(slots // 128)
        ],
        axis=0,
    )
    pick_row = iota((32, slots), 0)
    pick_slot = iota((32, slots), 1)
    pick = jnp.where(pick_row == owners, pick_slot % per_owner, 0)
    pick = jnp.where((pick_row < owners) & (pick_slot // per_owner == pick_row), 1, pick)
    found = nn_dot(pick.astype(F32).astype(BF16), held)
    stack = jnp.concatenate(
        [found[:owners, group * 128 : (group + 1) * 128] for group in range(groups)], axis=0
    )
    hot = stack.astype(BF16)
    stacked = groups * owners
    ranks = nn_dot(hot, as_mask(iota((128, 128), 0) < iota((128, 128), 1)))
    totals = nn_dot(hot, jnp.ones((128, 128), BF16)).astype(BF16)
    to_row, from_row = iota((stacked, stacked), 0), iota((stacked, stacked), 1)
    prior = as_mask((from_row // owners < to_row // owners) & (from_row % owners == to_row % owners))
    ranks = ranks + nn_dot(prior, totals)
    ranks = ranks + ((iota((stacked, 128), 0) % owners) * capacity).astype(F32)
    placed = stack * ranks
    targets = [
        jnp.sum(placed[group * owners : (group + 1) * owners], axis=0, keepdims=True).astype(
            jnp.int32
        )
        for group in range(groups)
    ]
    slot_columns = to_column(
        jnp.concatenate(
            [found[owners : owners + 1, group * 128 : (group + 1) * 128] for group in range(groups)],
            axis=0,
        )
    )

    positions = jnp.where(role == 0, position_ref[...], 0)
    position_columns = 32.0 * to_column((positions >> 5).astype(F32)) + to_column(
        (positions & 31).astype(F32)
    )
    lane = iota((128, 128), 1)

    whole_weight.wait()
    for group in range(2, depth):
        load(group).start()
    piece = 1024
    for group in range(groups):
        load(group).wait()
        product = jnp.zeros((128, 128), F32)
        total = jnp.zeros((128, 128), F32)
        for start in range(0, width, piece):
            raw = x_ref[group % depth, :, start : start + piece]
            squares = raw * raw
            part = squares[:, :128]
            for tile in range(1, piece // 128):
                part = part + squares[:, tile * 128 : (tile + 1) * 128]
            total = total + part.astype(F32)
            gained = raw.reshape(8, 16, piece) * spread_ref[:, start : start + piece][None]
            product = product + nn_dot(
                gained.reshape(128, piece), weight_ref[start : start + piece, :]
            )
        if group + depth < groups:
            load(group + depth).start()
        mean = jnp.sum(total, axis=1, keepdims=True) / width
        scaled = product * lax.rsqrt(mean + EPSILON) + bias_ref[...].astype(F32)
        angles = position_columns[:, group : group + 1] * freq_ref[...]
        quarter = jnp.floor(angles * (2.0 / math.pi) + 0.5)
        rest = angles - quarter * 1.5703125
        rest = rest - quarter * 4.837512969970703125e-4
        rest = rest - quarter * 7.54978995489188216e-8
        square = rest * rest
        sine = rest + rest * square * (
            -1.6666654611e-1 + square * (8.3321608736e-3 + square * -1.9515295891e-4)
        )
        cosine = (
            1.0
            - 0.5 * square
            + square
            * square
            * (
                4.166664568298827e-2
                + square * (-1.388731625493765e-3 + square * 2.443315711809948e-5)
            )
        )
        turn = quarter.astype(jnp.int32) + jnp.where(lane < 64, 1, 0)
        table = jnp.where((turn & 1) == 1, cosine, sine)
        table = jnp.where((turn & 2) == 2, -table, table)
        swapped = pltpu.roll(table, 64, axis=1)
        cosines = jnp.where(lane < 64, table, swapped)
        sines = jnp.where(lane < 64, -swapped, table)
        rotated = scaled * cosines + pltpu.roll(scaled, 64, axis=1) * sines
        span = slice(group * 128, (group + 1) * 128)
        rounded_ref[span, :128] = rotated.astype(BF16)
        rounded_ref[span, 128:] = jnp.broadcast_to(
            slot_columns[:, group : group + 1], (128, 128)
        ).astype(BF16)
        perm_ref[:, span] = as_mask(iota((rows, 128), 0) == targets[group])

    ordered = nn_dot(perm_ref[...], rounded_ref[...])
    diagonal = iota((128, 128), 0) == iota((128, 128), 1)
    lanes = iota((16, 128), 1)
    for owner in range(owners):
        span = slice(owner * capacity, (owner + 1) * capacity)
        place = owner * 2 % owners + owner * 2 // owners
        out_ref[place, :capacity, :] = ordered[span, :128].astype(BF16)
        if owner % 2 == 0:
            ids = ordered[owner * capacity : owner * capacity + 128, 128:]
            ids = jnp.sum(jnp.where(diagonal, ids, 0.0), axis=0, keepdims=True)
            both = jnp.broadcast_to(ids, (16, 128))
            other = pltpu.roll(both, 64, axis=1)
        mine = (lanes < 64) if owner % 2 == 0 else (lanes >= 64)
        out_ref[place, capacity:, :] = jnp.where(mine, both, other).astype(BF16)


def prefill(span_x, norm_gain, weight, bias, span_req, span_pos, members, owners):
    rows, width = span_x.shape
    head_dim = weight.shape[1]
    groups = rows // 128
    half = head_dim // 2
    depth = 4
    freq = (THETA_BASE ** (-(np.arange(head_dim) % half) / half)).astype(np.float32)[None, :]
    small = [
        norm_gain.reshape(-1, 128),
        bias,
        jnp.asarray(freq),
        span_req.reshape(-1, 128),
        span_pos.reshape(-1, 128),
        members.reshape(-1, 128),
    ]
    held = [small[0].shape, small[1].shape, small[2].shape]
    held += [(groups, 128), (groups, 128), small[5].shape]
    return pl.pallas_call(
        prefill_kernel,
        out_shape=jax.ShapeDtypeStruct((owners, rows // owners + 16, head_dim), BF16),
        in_specs=[pl.BlockSpec(memory_space=pl.ANY)] * 8,
        out_specs=pl.BlockSpec(memory_space=pltpu.VMEM),
        scratch_shapes=[
            pltpu.VMEM((depth, 128, width), BF16),
            pltpu.VMEM((width, head_dim), BF16),
        ]
        + [pltpu.VMEM(shape, array.dtype) for shape, array in zip(held, small)]
        + [
            pltpu.VMEM((16, width), BF16),
            pltpu.VMEM((rows, rows), BF16),
            pltpu.VMEM((rows, 2 * head_dim), BF16),
            pltpu.SemaphoreType.DMA((depth,)),
            pltpu.SemaphoreType.DMA,
            pltpu.SemaphoreType.DMA((len(small),)),
        ],
        compiler_params=pltpu.CompilerParams(vmem_limit_bytes=60 * MIB),
        cost_estimate=pl.CostEstimate(
            flops=2 * rows * width * head_dim, bytes_accessed=2 * rows * width, transcendentals=0
        ),
        name="prefill",
    )(span_x, weight, *small)


def attention_kernel(
    members, cache_len, query_ref, cache_ref, fresh_ref, row_ref, out_ref, q_ref, s_ref, p_ref, sum_ref, acc_ref
):
    place = (lax.axis_index("role"), lax.axis_index("batch"))
    steps, slots, heads, dim = query_ref.shape
    per_slot = steps * heads
    rows = slots * per_slot
    cached = cache_ref.shape[1]
    blocks = row_ref.shape[0] // 2
    capacity = row_ref.shape[1] - 16
    spanned = blocks * capacity
    newest = fresh_ref.shape[0]
    scale = 1.0 / math.sqrt(dim)
    for slot in range(slots):
        q_ref[slot * per_slot : (slot + 1) * per_slot, :] = jnp.concatenate(
            [query_ref[step, slot].astype(F32) for step in range(steps)], axis=0
        ).astype(BF16)
    column = iota((per_slot, cached), 1)
    for slot in range(slots):
        span = pl.ds(slot * per_slot, per_slot)
        scores = nt_dot(q_ref[span, :], cache_ref[slot]) * scale
        owner = place[0] * (members.shape[0] // slots // 2) + place[1]
        length = cache_len[members[owner * slots + slot]]
        keep = ((column & 1) == 0) & (column < 2 * length)
        s_ref[span, :cached] = jnp.where(keep, scores, NEGATIVE)
    keys = [row_ref[2 * block, :capacity, :] for block in range(blocks)]
    values = [row_ref[2 * block + 1, :capacity, :] for block in range(blocks)]
    lane = iota((16, 128), 1)
    row_slot = iota((rows, 128), 0) // per_slot
    for pair in range(spanned // 128):
        scores = nt_dot(q_ref[...], jnp.concatenate(keys[2 * pair : 2 * pair + 2], axis=0)) * scale
        left = row_ref[4 * pair, capacity:, :].astype(F32)
        right = row_ref[4 * pair + 2, capacity:, :].astype(F32)
        ids = jnp.where(lane < 64, left, right)[0:1].astype(jnp.int32)
        s_ref[:, cached + pair * 128 : cached + (pair + 1) * 128] = jnp.where(
            row_slot == ids, scores, NEGATIVE
        )
    row = iota((rows, newest), 0)
    col = iota((rows, newest), 1)
    per_step = 2 * slots
    keep = (
        ((col & 1) == 0)
        & ((col % per_step) // 2 == row // per_slot)
        & (col // per_step <= (row % per_slot) // heads)
    )
    scores = nt_dot(q_ref[...], fresh_ref[...]) * scale
    s_ref[:, cached + spanned :] = jnp.where(keep, scores, NEGATIVE)
    for slot in range(slots):
        span = pl.ds(slot * per_slot, per_slot)
        scores = s_ref[span, :]
        top = jnp.max(scores, axis=1, keepdims=True)
        weights = jnp.exp(scores - top)
        sum_ref[span, :] = jnp.broadcast_to(jnp.sum(weights, axis=1, keepdims=True), (per_slot, dim))
        p_ref[span, :cached] = pltpu.roll(weights[:, :cached], 1, axis=1).astype(BF16)
        p_ref[span, cached : cached + spanned] = weights[:, cached : cached + spanned].astype(BF16)
        p_ref[span, cached + spanned :] = pltpu.roll(
            weights[:, cached + spanned :], 1, axis=1
        ).astype(BF16)
    acc_ref[...] = nn_dot(
        p_ref[:, cached : cached + spanned], jnp.concatenate(values, axis=0)
    ) + nn_dot(p_ref[:, cached + spanned :], fresh_ref[...])
    for slot in range(slots):
        span = pl.ds(slot * per_slot, per_slot)
        acc_ref[span, :] = (
            acc_ref[span, :] + nn_dot(p_ref[span, :cached], cache_ref[slot])
        ) / sum_ref[span, :]
    for head in range(heads):
        out_ref[head] = acc_ref[pl.ds(head, slots * steps, stride=heads), :].astype(BF16)


def attend(members, cache_len, queries, cache, fresh, rows):
    steps, slots, heads, dim = queries.shape
    count = slots * steps * heads
    cached = cache.shape[1]
    spanned = (rows.shape[0] // 2) * (rows.shape[1] - 16)
    columns = cached + spanned + fresh.shape[0]
    vmem = pl.BlockSpec(memory_space=pltpu.VMEM)
    return pl.pallas_call(
        attention_kernel,
        out_shape=jax.ShapeDtypeStruct((heads, slots * steps, dim), BF16),
        in_specs=[pl.BlockSpec(memory_space=pltpu.SMEM)] * 2 + [vmem] * 4,
        out_specs=vmem,
        scratch_shapes=[
            pltpu.VMEM((count, dim), BF16),
            pltpu.VMEM((count, columns), F32),
            pltpu.VMEM((count, columns), BF16),
            pltpu.VMEM((count, dim), F32),
            pltpu.VMEM((count, dim), F32),
        ],
        compiler_params=pltpu.CompilerParams(vmem_limit_bytes=32 * MIB),
        name="attend",
    )(members, cache_len, queries, cache, fresh, rows)


AXES = ("role", "batch", "tensor")


def places(device):
    batch, tensor = device // 8 % 8, device % 8
    return device // 64, batch // 4, batch % 4, tensor // 2, tensor % 2


def moves(target):
    pairs = []
    for source in range(128):
        role, x_lo, z, y, x_hi = target(*places(source))
        pairs.append((source, role * 64 + (x_lo * 4 + z) * 8 + y * 2 + x_hi))
    return pairs


def sum_round(k):
    return moves(
        lambda role, x_lo, z, y, x_hi: (
            role,
            (y & 1) ^ (k & 1),
            z,
            2 * ((y >> 1) ^ (k >> 2)) + x_lo,
            x_hi ^ (k >> 1 & 1),
        )
    )


def project_kernel(mine_ref, other_ref, own_ref, x_ref, *rest):
    outs, staged = rest[:-1], rest[-1]
    role, batch, tensor = (lax.axis_index(name) for name in AXES)
    x_lo, z_top, z_low = batch >> 2, (batch >> 1) & 1, batch & 1
    y, x_hi = tensor >> 1, tensor & 1
    blocks, heads, rows, _ = mine_ref.shape
    for step, ref in enumerate((mine_ref, other_ref)):
        left = jnp.concatenate(
            [
                jnp.concatenate([ref[block, head] for head in range(heads)], axis=1)
                for block in range(blocks)
            ],
            axis=0,
        )
        for turn, weight in enumerate((own_ref, x_ref)):
            product = nn_dot(left, weight[...]).astype(BF16)
            for block in range(blocks):
                slot = 4 * (role ^ step ^ (y >> 1))
                slot += 2 * (z_top ^ (block >> 1) ^ x_hi) + (x_lo ^ turn ^ (y & 1))
                start = pl.multiple_of((z_low ^ (block & 1)) * rows, rows)
                staged[slot, pl.ds(start, rows), :] = product[block * rows : (block + 1) * rows]
    for turn, out in enumerate(outs):
        out[...] = staged[turn]


def project_out(mine, other, *weights):
    _, heads, rows, _ = mine.shape
    columns = weights[0].shape[1]
    vmem = pl.BlockSpec(memory_space=pltpu.VMEM)
    return pl.pallas_call(
        project_kernel,
        out_shape=[jax.ShapeDtypeStruct((2 * rows, columns), BF16)] * 8,
        in_specs=[vmem] * 4,
        out_specs=[vmem] * 8,
        scratch_shapes=[pltpu.VMEM((8, 2 * rows, columns), BF16)],
        compiler_params=pltpu.CompilerParams(vmem_limit_bytes=32 * MIB),
        name="project_out",
    )(mine, other, *weights)


def add_kernel(*refs):
    out_ref = refs[-1]
    total = refs[0][...].astype(F32)
    for ref in refs[1:-1]:
        total = total + ref[...].astype(F32)
    out_ref[...] = total.reshape(out_ref.shape).astype(BF16)


def add_up(parts, steps):
    rows, columns = parts[0].shape
    vmem = pl.BlockSpec(memory_space=pltpu.VMEM)
    return pl.pallas_call(
        add_kernel,
        out_shape=jax.ShapeDtypeStruct((rows // steps, steps, columns), BF16),
        in_specs=[vmem] * len(parts),
        out_specs=vmem,
        compiler_params=pltpu.CompilerParams(vmem_limit_bytes=32 * MIB),
        name="add_up",
    )(*parts)


def body(
    span_x,
    norm_gain,
    key_value_weight,
    key_value_bias,
    queries,
    decode_key_value,
    kv_cache,
    w_out,
    members,
    span_req,
    span_pos,
    cache_len,
):
    n_role = lax.axis_size("role")
    n_batch = lax.axis_size("batch")
    owners = n_role * n_batch
    width = span_x.shape[1]
    head_dim = key_value_weight.shape[3]
    steps, slots, heads, _ = queries.shape
    beside = lax.ppermute(w_out, "batch", [(b, b ^ 4) for b in range(8)])
    outgoing = prefill(
        span_x,
        norm_gain,
        key_value_weight.reshape(width, head_dim),
        key_value_bias.reshape(1, head_dim),
        span_req,
        span_pos,
        members,
        owners,
    )
    arrived = lax.all_to_all(outgoing, ("batch", "role"), 0, 0)
    arrived, beside = lax.optimization_barrier((arrived, beside))
    attention = attend(
        members,
        cache_len,
        queries,
        kv_cache.reshape(slots, -1, head_dim),
        decode_key_value.reshape(-1, head_dim),
        arrived,
    )

    gathered = jnp.stack(
        [attention]
        + [lax.ppermute(attention, "batch", [(b, b ^ k) for b in range(8)]) for k in range(1, 4)]
    )
    other = lax.ppermute(gathered, "role", [(0, 1), (1, 0)])
    parts = project_out(gathered, other, w_out, beside)
    return add_up([lax.ppermute(parts[k], AXES, sum_round(k)) for k in range(8)], steps)


def solution(mesh):
    placed = (
        P("batch", None),
        P(),
        P(None, "tensor", "role", None),
        P("tensor", "role", None),
        P(None, ("role", "batch"), "tensor", None),
        P(None, ("role", "batch"), "tensor", None, None),
        P(("role", "batch"), None, "tensor", None, None),
        P("tensor", ("role", "batch")),
        P(),
        P(),
        P(),
        P(),
    )
    return jax.shard_map(
        body,
        mesh=mesh,
        in_specs=placed,
        out_specs=P("tensor", None, ("role", "batch")),
        check_vma=False,
    )
```

```python
import functools
import math

import jax
import jax.numpy as jnp
import numpy as np
from jax import lax
from jax.experimental import pallas as pl
from jax.experimental.pallas import tpu as pltpu
from jax.sharding import PartitionSpec as P

EPSILON = 1e-06
THETA_BASE = 1000000.0
NEGATIVE = -1e30
F32 = jnp.float32
BF16 = jnp.bfloat16
MIB = 1024 * 1024


def nt_dot(a, b):
    return lax.dot_general(a, b, (((1,), (1,)), ((), ())), preferred_element_type=F32)


def nn_dot(a, b):
    return jnp.dot(a, b, preferred_element_type=F32)


def iota(shape, dim):
    return lax.broadcasted_iota(jnp.int32, shape, dim)


def as_mask(cond, dtype=BF16):
    return jnp.where(cond, 1.0, 0.0).astype(dtype)


def to_column(rows):
    eye = as_mask(iota((128, 128), 0) == iota((128, 128), 1))
    return nt_dot(eye, rows.astype(BF16))


def prefill_kernel(
    x_hbm,
    weight_hbm,
    gain_hbm,
    bias_hbm,
    freq_hbm,
    request_hbm,
    position_hbm,
    member_hbm,
    out_ref,
    x_ref,
    weight_ref,
    gain_ref,
    bias_ref,
    freq_ref,
    request_ref,
    position_ref,
    member_ref,
    spread_ref,
    perm_ref,
    rounded_ref,
    x_sem,
    weight_sem,
    small_sem,
):
    role, batch = lax.axis_index("role"), lax.axis_index("batch")
    rows, width = x_hbm.shape
    depth = x_ref.shape[0]
    owners = out_ref.shape[0]
    capacity = rows // owners
    groups = rows // 128
    slots = member_ref.shape[0] * 128
    per_owner = slots // owners

    block = pl.ds(pl.multiple_of(batch * groups, 8), groups)
    small = [
        pltpu.make_async_copy(source, target, small_sem.at[index])
        for index, (source, target) in enumerate(
            [
                (member_hbm, member_ref),
                (request_hbm.at[block, :], request_ref),
                (gain_hbm, gain_ref),
                (position_hbm.at[block, :], position_ref),
                (bias_hbm, bias_ref),
                (freq_hbm, freq_ref),
            ]
        )
    ]
    for copy in small:
        copy.start()
    whole_weight = pltpu.make_async_copy(weight_hbm, weight_ref, weight_sem)
    whole_weight.start()

    def load(group):
        return pltpu.make_async_copy(
            x_hbm.at[pl.ds(group * 128, 128), :], x_ref.at[group % depth], x_sem.at[group % depth]
        )

    for group in range(2):
        load(group).start()
    for copy in small:
        copy.wait()

    for tile in range(width // 128):
        spread_ref[:, tile * 128 : (tile + 1) * 128] = jnp.broadcast_to(
            gain_ref[tile : tile + 1, :], (16, 128)
        )

    members = member_ref[...]
    filler = jnp.zeros((8 - members.shape[0], 128), jnp.int32)
    turned = to_column(jnp.concatenate([members, filler], axis=0).astype(F32))
    requests = request_ref[...].astype(F32)
    held = jnp.concatenate(
        [
            jnp.concatenate(
                [
                    as_mask(turned[:, part : part + 1] == requests[group : group + 1, :])
                    for group in range(groups)
                ],
                axis=1,
            )
            for part in range(slots // 128)
        ],
        axis=0,
    )
    pick_row = iota((32, slots), 0)
    pick_slot = iota((32, slots), 1)
    pick = jnp.where(pick_row == owners, pick_slot % per_owner, 0)
    pick = jnp.where((pick_row < owners) & (pick_slot // per_owner == pick_row), 1, pick)
    found = nn_dot(pick.astype(F32).astype(BF16), held)
    stack = jnp.concatenate(
        [found[:owners, group * 128 : (group + 1) * 128] for group in range(groups)], axis=0
    )
    hot = stack.astype(BF16)
    stacked = groups * owners
    ranks = nn_dot(hot, as_mask(iota((128, 128), 0) < iota((128, 128), 1)))
    totals = nn_dot(hot, jnp.ones((128, 128), BF16)).astype(BF16)
    to_row, from_row = iota((stacked, stacked), 0), iota((stacked, stacked), 1)
    prior = as_mask((from_row // owners < to_row // owners) & (from_row % owners == to_row % owners))
    ranks = ranks + nn_dot(prior, totals)
    ranks = ranks + ((iota((stacked, 128), 0) % owners) * capacity).astype(F32)
    placed = stack * ranks
    targets = [
        jnp.sum(placed[group * owners : (group + 1) * owners], axis=0, keepdims=True).astype(
            jnp.int32
        )
        for group in range(groups)
    ]
    slot_columns = to_column(
        jnp.concatenate(
            [found[owners : owners + 1, group * 128 : (group + 1) * 128] for group in range(groups)],
            axis=0,
        )
    )

    positions = jnp.where(role == 0, position_ref[...], 0)
    position_columns = 32.0 * to_column((positions >> 5).astype(F32)) + to_column(
        (positions & 31).astype(F32)
    )
    lane = iota((128, 128), 1)

    whole_weight.wait()
    for group in range(2, depth):
        load(group).start()
    piece = 1024
    for group in range(groups):
        load(group).wait()
        product = jnp.zeros((128, 128), F32)
        total = jnp.zeros((128, 128), F32)
        for start in range(0, width, piece):
            raw = x_ref[group % depth, :, start : start + piece]
            squares = raw * raw
            part = squares[:, :128]
            for tile in range(1, piece // 128):
                part = part + squares[:, tile * 128 : (tile + 1) * 128]
            total = total + part.astype(F32)
            gained = raw.reshape(8, 16, piece) * spread_ref[:, start : start + piece][None]
            product = product + nn_dot(
                gained.reshape(128, piece), weight_ref[start : start + piece, :]
            )
        if group + depth < groups:
            load(group + depth).start()
        mean = jnp.sum(total, axis=1, keepdims=True) / width
        scaled = product * lax.rsqrt(mean + EPSILON) + bias_ref[...].astype(F32)
        angles = position_columns[:, group : group + 1] * freq_ref[...]
        quarter = jnp.floor(angles * (2.0 / math.pi) + 0.5)
        rest = angles - quarter * 1.5703125
        rest = rest - quarter * 4.837512969970703125e-4
        rest = rest - quarter * 7.54978995489188216e-8
        square = rest * rest
        sine = rest + rest * square * (
            -1.6666654611e-1 + square * (8.3321608736e-3 + square * -1.9515295891e-4)
        )
        cosine = (
            1.0
            - 0.5 * square
            + square
            * square
            * (
                4.166664568298827e-2
                + square * (-1.388731625493765e-3 + square * 2.443315711809948e-5)
            )
        )
        turn = quarter.astype(jnp.int32) + jnp.where(lane < 64, 1, 0)
        table = jnp.where((turn & 1) == 1, cosine, sine)
        table = jnp.where((turn & 2) == 2, -table, table)
        swapped = pltpu.roll(table, 64, axis=1)
        cosines = jnp.where(lane < 64, table, swapped)
        sines = jnp.where(lane < 64, -swapped, table)
        rotated = scaled * cosines + pltpu.roll(scaled, 64, axis=1) * sines
        span = slice(group * 128, (group + 1) * 128)
        rounded_ref[span, :128] = rotated.astype(BF16)
        rounded_ref[span, 128:] = jnp.broadcast_to(
            slot_columns[:, group : group + 1], (128, 128)
        ).astype(BF16)
        perm_ref[:, span] = as_mask(iota((rows, 128), 0) == targets[group])

    ordered = nn_dot(perm_ref[...], rounded_ref[...])
    diagonal = iota((128, 128), 0) == iota((128, 128), 1)
    lanes = iota((16, 128), 1)
    for owner in range(owners):
        span = slice(owner * capacity, (owner + 1) * capacity)
        place = owner * 2 % owners + owner * 2 // owners
        out_ref[place, :capacity, :] = ordered[span, :128].astype(BF16)
        if owner % 2 == 0:
            ids = ordered[owner * capacity : owner * capacity + 128, 128:]
            ids = jnp.sum(jnp.where(diagonal, ids, 0.0), axis=0, keepdims=True)
            both = jnp.broadcast_to(ids, (16, 128))
            other = pltpu.roll(both, 64, axis=1)
        mine = (lanes < 64) if owner % 2 == 0 else (lanes >= 64)
        out_ref[place, capacity:, :] = jnp.where(mine, both, other).astype(BF16)


def prefill(span_x, norm_gain, weight, bias, span_req, span_pos, members, owners):
    rows, width = span_x.shape
    head_dim = weight.shape[1]
    groups = rows // 128
    half = head_dim // 2
    depth = 4
    freq = (THETA_BASE ** (-(np.arange(head_dim) % half) / half)).astype(np.float32)[None, :]
    small = [
        norm_gain.reshape(-1, 128),
        bias,
        jnp.asarray(freq),
        span_req.reshape(-1, 128),
        span_pos.reshape(-1, 128),
        members.reshape(-1, 128),
    ]
    held = [small[0].shape, small[1].shape, small[2].shape]
    held += [(groups, 128), (groups, 128), small[5].shape]
    return pl.pallas_call(
        prefill_kernel,
        out_shape=jax.ShapeDtypeStruct((owners, rows // owners + 16, head_dim), BF16),
        in_specs=[pl.BlockSpec(memory_space=pl.ANY)] * 8,
        out_specs=pl.BlockSpec(memory_space=pltpu.VMEM),
        scratch_shapes=[
            pltpu.VMEM((depth, 128, width), BF16),
            pltpu.VMEM((width, head_dim), BF16),
        ]
        + [pltpu.VMEM(shape, array.dtype) for shape, array in zip(held, small)]
        + [
            pltpu.VMEM((16, width), BF16),
            pltpu.VMEM((rows, rows), BF16),
            pltpu.VMEM((rows, 2 * head_dim), BF16),
            pltpu.SemaphoreType.DMA((depth,)),
            pltpu.SemaphoreType.DMA,
            pltpu.SemaphoreType.DMA((len(small),)),
        ],
        compiler_params=pltpu.CompilerParams(vmem_limit_bytes=60 * MIB),
        cost_estimate=pl.CostEstimate(
            flops=2 * rows * width * head_dim, bytes_accessed=2 * rows * width, transcendentals=0
        ),
        name="prefill",
    )(span_x, weight, *small)


def attention_kernel(
    members, cache_len, query_ref, cache_ref, fresh_ref, row_ref, out_ref, q_ref, s_ref, p_ref, sum_ref, acc_ref
):
    place = (lax.axis_index("role"), lax.axis_index("batch"))
    steps, slots, heads, dim = query_ref.shape
    per_slot = steps * heads
    rows = slots * per_slot
    cached = cache_ref.shape[1]
    blocks = row_ref.shape[0] // 2
    capacity = row_ref.shape[1] - 16
    spanned = blocks * capacity
    newest = fresh_ref.shape[0]
    scale = 1.0 / math.sqrt(dim)
    for slot in range(slots):
        q_ref[slot * per_slot : (slot + 1) * per_slot, :] = jnp.concatenate(
            [query_ref[step, slot].astype(F32) for step in range(steps)], axis=0
        ).astype(BF16)
    column = iota((per_slot, cached), 1)
    for slot in range(slots):
        span = pl.ds(slot * per_slot, per_slot)
        scores = nt_dot(q_ref[span, :], cache_ref[slot]) * scale
        owner = place[0] * (members.shape[0] // slots // 2) + place[1]
        length = cache_len[members[owner * slots + slot]]
        keep = ((column & 1) == 0) & (column < 2 * length)
        s_ref[span, :cached] = jnp.where(keep, scores, NEGATIVE)
    keys = [row_ref[2 * block, :capacity, :] for block in range(blocks)]
    values = [row_ref[2 * block + 1, :capacity, :] for block in range(blocks)]
    lane = iota((16, 128), 1)
    row_slot = iota((rows, 128), 0) // per_slot
    for pair in range(spanned // 128):
        scores = nt_dot(q_ref[...], jnp.concatenate(keys[2 * pair : 2 * pair + 2], axis=0)) * scale
        left = row_ref[4 * pair, capacity:, :].astype(F32)
        right = row_ref[4 * pair + 2, capacity:, :].astype(F32)
        ids = jnp.where(lane < 64, left, right)[0:1].astype(jnp.int32)
        s_ref[:, cached + pair * 128 : cached + (pair + 1) * 128] = jnp.where(
            row_slot == ids, scores, NEGATIVE
        )
    row = iota((rows, newest), 0)
    col = iota((rows, newest), 1)
    per_step = 2 * slots
    keep = (
        ((col & 1) == 0)
        & ((col % per_step) // 2 == row // per_slot)
        & (col // per_step <= (row % per_slot) // heads)
    )
    scores = nt_dot(q_ref[...], fresh_ref[...]) * scale
    s_ref[:, cached + spanned :] = jnp.where(keep, scores, NEGATIVE)
    for slot in range(slots):
        span = pl.ds(slot * per_slot, per_slot)
        scores = s_ref[span, :]
        top = jnp.max(scores, axis=1, keepdims=True)
        weights = jnp.exp(scores - top)
        sum_ref[span, :] = jnp.broadcast_to(jnp.sum(weights, axis=1, keepdims=True), (per_slot, dim))
        p_ref[span, :cached] = pltpu.roll(weights[:, :cached], 1, axis=1).astype(BF16)
        p_ref[span, cached : cached + spanned] = weights[:, cached : cached + spanned].astype(BF16)
        p_ref[span, cached + spanned :] = pltpu.roll(
            weights[:, cached + spanned :], 1, axis=1
        ).astype(BF16)
    acc_ref[...] = nn_dot(
        p_ref[:, cached : cached + spanned], jnp.concatenate(values, axis=0)
    ) + nn_dot(p_ref[:, cached + spanned :], fresh_ref[...])
    for slot in range(slots):
        span = pl.ds(slot * per_slot, per_slot)
        acc_ref[span, :] = (
            acc_ref[span, :] + nn_dot(p_ref[span, :cached], cache_ref[slot])
        ) / sum_ref[span, :]
    for head in range(heads):
        out_ref[head] = acc_ref[pl.ds(head, slots * steps, stride=heads), :].astype(BF16)


def attend(members, cache_len, queries, cache, fresh, rows):
    steps, slots, heads, dim = queries.shape
    count = slots * steps * heads
    cached = cache.shape[1]
    spanned = (rows.shape[0] // 2) * (rows.shape[1] - 16)
    columns = cached + spanned + fresh.shape[0]
    vmem = pl.BlockSpec(memory_space=pltpu.VMEM)
    return pl.pallas_call(
        attention_kernel,
        out_shape=jax.ShapeDtypeStruct((heads, slots * steps, dim), BF16),
        in_specs=[pl.BlockSpec(memory_space=pltpu.SMEM)] * 2 + [vmem] * 4,
        out_specs=vmem,
        scratch_shapes=[
            pltpu.VMEM((count, dim), BF16),
            pltpu.VMEM((count, columns), F32),
            pltpu.VMEM((count, columns), BF16),
            pltpu.VMEM((count, dim), F32),
            pltpu.VMEM((count, dim), F32),
        ],
        compiler_params=pltpu.CompilerParams(vmem_limit_bytes=32 * MIB),
        name="attend",
    )(members, cache_len, queries, cache, fresh, rows)


AXES = ("role", "batch", "tensor")


def places(device):
    batch, tensor = device // 8 % 8, device % 8
    return device // 64, batch // 4, batch % 4, tensor // 2, tensor % 2


def moves(target):
    pairs = []
    for source in range(128):
        role, x_lo, z, y, x_hi = target(*places(source))
        pairs.append((source, role * 64 + (x_lo * 4 + z) * 8 + y * 2 + x_hi))
    return pairs


def sum_round(k):
    return moves(
        lambda role, x_lo, z, y, x_hi: (
            role,
            (y & 1) ^ (k & 1),
            z,
            2 * ((y >> 1) ^ (k >> 2)) + x_lo,
            x_hi ^ (k >> 1 & 1),
        )
    )


def project_kernel(mine_ref, other_ref, own_ref, x_ref, *rest):
    outs, staged = rest[:-1], rest[-1]
    role, batch, tensor = (lax.axis_index(name) for name in AXES)
    x_lo, z_top, z_low = batch >> 2, (batch >> 1) & 1, batch & 1
    y, x_hi = tensor >> 1, tensor & 1
    blocks, heads, rows, _ = mine_ref.shape
    for step, ref in enumerate((mine_ref, other_ref)):
        left = jnp.concatenate(
            [
                jnp.concatenate([ref[block, head] for head in range(heads)], axis=1)
                for block in range(blocks)
            ],
            axis=0,
        )
        for turn, weight in enumerate((own_ref, x_ref)):
            product = nn_dot(left, weight[...]).astype(BF16)
            for block in range(blocks):
                slot = 4 * (role ^ step ^ (y >> 1))
                slot += 2 * (z_top ^ (block >> 1) ^ x_hi) + (x_lo ^ turn ^ (y & 1))
                start = pl.multiple_of((z_low ^ (block & 1)) * rows, rows)
                staged[slot, pl.ds(start, rows), :] = product[block * rows : (block + 1) * rows]
    for turn, out in enumerate(outs):
        out[...] = staged[turn]


def project_out(mine, other, *weights):
    _, heads, rows, _ = mine.shape
    columns = weights[0].shape[1]
    vmem = pl.BlockSpec(memory_space=pltpu.VMEM)
    return pl.pallas_call(
        project_kernel,
        out_shape=[jax.ShapeDtypeStruct((2 * rows, columns), BF16)] * 8,
        in_specs=[vmem] * 4,
        out_specs=[vmem] * 8,
        scratch_shapes=[pltpu.VMEM((8, 2 * rows, columns), BF16)],
        compiler_params=pltpu.CompilerParams(vmem_limit_bytes=32 * MIB),
        name="project_out",
    )(mine, other, *weights)


def add_kernel(*refs):
    out_ref = refs[-1]
    total = refs[0][...].astype(F32)
    for ref in refs[1:-1]:
        total = total + ref[...].astype(F32)
    out_ref[...] = total.reshape(out_ref.shape).astype(BF16)


def add_up(parts, steps):
    rows, columns = parts[0].shape
    vmem = pl.BlockSpec(memory_space=pltpu.VMEM)
    return pl.pallas_call(
        add_kernel,
        out_shape=jax.ShapeDtypeStruct((rows // steps, steps, columns), BF16),
        in_specs=[vmem] * len(parts),
        out_specs=vmem,
        compiler_params=pltpu.CompilerParams(vmem_limit_bytes=32 * MIB),
        name="add_up",
    )(*parts)


def body(
    span_x,
    norm_gain,
    key_value_weight,
    key_value_bias,
    queries,
    decode_key_value,
    kv_cache,
    w_out,
    members,
    span_req,
    span_pos,
    cache_len,
):
    n_role = lax.axis_size("role")
    n_batch = lax.axis_size("batch")
    owners = n_role * n_batch
    width = span_x.shape[1]
    head_dim = key_value_weight.shape[3]
    steps, slots, heads, _ = queries.shape
    beside = lax.ppermute(w_out, "batch", [(b, b ^ 4) for b in range(8)])
    outgoing = prefill(
        span_x,
        norm_gain,
        key_value_weight.reshape(width, head_dim),
        key_value_bias.reshape(1, head_dim),
        span_req,
        span_pos,
        members,
        owners,
    )
    arrived = lax.all_to_all(outgoing, ("batch", "role"), 0, 0)
    arrived, beside = lax.optimization_barrier((arrived, beside))
    attention = attend(
        members,
        cache_len,
        queries,
        kv_cache.reshape(slots, -1, head_dim),
        decode_key_value.reshape(-1, head_dim),
        arrived,
    )

    gathered = jnp.stack(
        [attention]
        + [lax.ppermute(attention, "batch", [(b, b ^ k) for b in range(8)]) for k in range(1, 4)]
    )
    other = lax.ppermute(gathered, "role", [(0, 1), (1, 0)])
    parts = project_out(gathered, other, w_out, beside)
    order = (0, 1, 3, 2, 6, 7, 5, 4)
    return add_up([lax.ppermute(parts[k], AXES, sum_round(k)) for k in order], steps)


def solution(mesh):
    placed = (
        P("batch", None),
        P(),
        P(None, "tensor", "role", None),
        P("tensor", "role", None),
        P(None, ("role", "batch"), "tensor", None),
        P(None, ("role", "batch"), "tensor", None, None),
        P(("role", "batch"), None, "tensor", None, None),
        P("tensor", ("role", "batch")),
        P(),
        P(),
        P(),
        P(),
    )
    return jax.shard_map(
        body,
        mesh=mesh,
        in_specs=placed,
        out_specs=P("tensor", None, ("role", "batch")),
        check_vma=False,
    )
```
